256 devices in a mesh: rows: 64 (over z, y, x_hi), feat: 4 (over x_lo, core).
Axes of the slice: x: 4 (x_hi: 2, x_lo: 2; x = x_hi * 2 + x_lo), y: 4, z: 8, core: 2. Of those that a mesh axis runs over, the one named last changes fastest.
Arguments:
- query_grads: bfloat16 [1024, 8192], P('rows', 'feat'), may hold values from -300 to 300
- train_grads: bfloat16 [65536, 8192], P('rows', 'feat'), may hold values from -300 to 300
- precond: bfloat16 [32, 256, 256], P('feat'), may hold values from -1.1 to 4.1, as said below
Outputs:
- scores: float32 [1024, 65536], P(None, ('rows', 'feat'))
The draws below stay inside these ranges and needn't reach their ends.
Inputs may be any that keep to these rules, and one draw needn't show every extreme that they name: `precond`: each block is symmetric.
All inputs are finite; a program needn't handle non-finite values.
Results may differ from the reference program's by a relative error of at most 0.003.
Values may be sent and summed in bfloat16 or wider, within the bound.
No kernel may reach another device: no remote copies, remote signals or barrier semaphores. Data moves between devices by JAX's collectives and lax.ppermute only.
A program may use at most 64 MiB of HBM per device.

```python
import math
import jax
import jax.numpy as jnp
from jax import lax

F = 8192
BS = 256
NBLK = 32
TR_DEV = 1024
Q = 1024
N = 65536
N_ROWS = 64


def column_scales(key, extent, growth):
    ramp = growth ** (jnp.arange(extent, dtype=jnp.float32) / extent)
    return ramp * jnp.exp(jax.random.uniform(key, (extent,), jnp.float32, 0.0, math.log(10.0)))


def row_scales(key, number):
    return jnp.exp(jax.random.uniform(key, (number, 1), jnp.float32, 0.0, math.log(10.0)))


def draw_query_grads(key, part):
    key = jax.random.fold_in(key, 11)
    subkeys = jax.random.split(key, 4)
    entries = jnp.clip(jax.random.normal(subkeys[0], (Q, F), jnp.float32), -6.0, 6.0)
    growth = 3.0
    values = 0.1 * entries * column_scales(subkeys[2], F, growth) * row_scales(subkeys[3], Q)
    return values.astype(jnp.bfloat16)


def draw_train_grads(key, part):
    key = jax.random.fold_in(key, 12)
    subkeys = jax.random.split(key, 4)
    entries = jnp.clip(jax.random.normal(subkeys[0], (N, F), jnp.float32), -6.0, 6.0)
    growth = 3.0
    values = 0.1 * entries * column_scales(subkeys[2], F, growth) * row_scales(subkeys[3], N)
    return values.astype(jnp.bfloat16)


def draw_precond(key, part):
    key = jax.random.fold_in(key, 13)
    subkeys = jax.random.split(key, 2)
    diagonal = jax.random.uniform(subkeys[0], (NBLK, BS, 1), jnp.float32, 1.0, 3.0)
    entries = jnp.clip(jax.random.normal(subkeys[1], (NBLK, BS, BS), jnp.float32), -6.0, 6.0)
    symmetric = (entries + jnp.swapaxes(entries, 1, 2)) * (0.5 / math.sqrt(BS))
    identity = (jnp.arange(BS)[:, None] == jnp.arange(BS)[None, :]).astype(jnp.float32)
    return (symmetric + diagonal * identity).astype(jnp.bfloat16)


def setup_inputs(seed: int = 0) -> dict:
    arg_keys = jax.random.split(jax.random.key(seed), 4)
    query_grads = draw_query_grads(jax.random.fold_in(arg_keys[3], 71), 0)
    train_grads = draw_train_grads(jax.random.fold_in(arg_keys[3], 71), 0)
    precond = draw_precond(jax.random.fold_in(arg_keys[3], 71), 0)
    return dict(query_grads=query_grads, train_grads=train_grads, precond=precond)


eps = 1e-06

def reference(query_grads, train_grads, precond):
    shaped = query_grads.astype(jnp.float32).reshape(Q, NBLK, BS)
    conditioned = jnp.einsum('qkb,kbc->qkc', shaped, precond.astype(jnp.float32), precision=lax.Precision.HIGHEST).reshape(Q, F)
    query_scale = 1.0 / jnp.sqrt(lax.optimization_barrier(jnp.sum(conditioned * conditioned, axis=1)) + eps)
    narrowed = lax.optimization_barrier(conditioned.astype(jnp.bfloat16))
    rounded = narrowed.astype(jnp.float32)
    factor = math.sqrt(F)
    stacked = train_grads.reshape(N_ROWS, TR_DEV, F)

    def score_block(train_block):
        widened = train_block.astype(jnp.float32)
        train_scale = 1.0 / jnp.sqrt(lax.optimization_barrier(jnp.sum(widened * widened, axis=1)) + eps)
        products = jnp.dot(rounded, widened.T, precision=lax.Precision.HIGHEST, preferred_element_type=jnp.float32)
        return products * query_scale[:, None] * train_scale[None, :] * factor
    blocks = lax.map(score_block, stacked)
    return jnp.transpose(blocks, (1, 0, 2)).reshape(Q, N)
```

```python
import math

import jax
import jax.numpy as jnp
from jax import lax
from jax.experimental import pallas as pl
from jax.experimental.pallas import tpu as pltpu
from jax.sharding import PartitionSpec as P

F = 8192
EPS = 1e-06
NZ, NY, NX = 8, 4, 2
SHARD = 16
BLOCK = 4 * SHARD
NEAR = (0, -1, 1, -2)
VMEM = pl.BlockSpec(memory_space=pltpu.VMEM)
SMEM = pl.BlockSpec(memory_space=pltpu.SMEM)
MIB = 1 << 20


def row_index(z, y, x):
    return (z % NZ) * (NY * NX) + (y % NY) * NX + x % NX


def shift(value, even, odd=None):
    odd = even if odd is None else odd
    pairs = []
    for z in range(NZ):
        for y in range(NY):
            for x in range(NX):
                for f in range(4):
                    dz, dy, dx = odd if f % 2 else even
                    there = row_index(z + dz, y + dy, x + dx)
                    pairs.append((row_index(z, y, x) * 4 + f, there * 4 + f))
    return lax.ppermute(value, ("rows", "feat"), pairs)


def across(value, mask):
    return lax.ppermute(value, "feat", [(f, f ^ mask) for f in range(4)])


def join(*parts):
    return jnp.concatenate(parts, axis=0)


def gather(own):
    pair = join(own, shift(own, (4, 0, 0)))
    four = join(pair, shift(pair, (0, 0, 1)))
    first = [
        shift(four, (0, 1, 0), (1, 0, 0)),
        shift(four, (0, -1, 0), (-1, 0, 0)),
        shift(four, (0, 2, 0), (2, 0, 0)),
    ]
    held = join(four, *first)
    before = shift(held, (1, 0, 0), (0, 1, 0))
    after = shift(held, (-1, 0, 0), (0, -1, 0))
    low = shift(held[: 2 * BLOCK], (2, 0, 0), (0, 2, 0))
    high = shift(held[2 * BLOCK :], (-2, 0, 0), (0, -2, 0))
    return held, before, after, low, high


PIECES = (
    tuple((a, 0) for a in NEAR),
    tuple((a, -1) for a in NEAR),
    tuple((a, 1) for a in NEAR),
    tuple((a, -2) for a in NEAR[:2]),
    tuple((a, 2) for a in NEAR[2:]),
)


def first_row(place, core, first, last, part):
    z, y, x = place[0], place[1], place[2]
    dz = jnp.where(core == 0, last, first)
    dy = jnp.where(core == 0, first, last)
    zz = lax.rem(z + dz + (4 * (part % 2) + NZ), NZ)
    yy = lax.rem(y + dy + NY, NY)
    xx = lax.rem(x + part // 2, NX)
    return pl.multiple_of((zz * (NY * NX) + yy * NX + xx) * SHARD, SHARD)


def split3(value):
    high = value.astype(jnp.bfloat16)
    rest = value - high.astype(jnp.float32)
    middle = rest.astype(jnp.bfloat16)
    low = (rest - middle.astype(jnp.float32)).astype(jnp.bfloat16)
    return [high, middle, low]


def prepare_kernel(place, train_ref, turned_ref, sums_ref):
    me = place[3]
    for k, mask in enumerate((0, 2, 1, 3)):
        start = pl.multiple_of((me ^ mask) * 256, 256)
        for j in range(0, 2048, 512):
            block = train_ref[pl.ds(start, 256), j : j + 512].T
            turned_ref[k, j : j + 512, :] = block
            wide = block.astype(jnp.float32)
            part = jnp.sum(wide * wide, axis=0, keepdims=True)
            if j == 0:
                sums_ref[k : k + 1, :] = part
            else:
                sums_ref[k : k + 1, :] += part


def products_kernel(place, turned_ref, precond_ref, *refs):
    pieces = refs[: len(PIECES)]
    keep_ref, send_ref, sums_ref, rounded_ref = refs[len(PIECES) :]
    core = place[3] % 2
    for piece, blocks in zip(pieces, PIECES):
        rows = piece.shape[0]
        squares = jnp.zeros((rows, 128), jnp.float32)
        for k in range(8):
            columns = slice(k * 256, (k + 1) * 256)
            value = jnp.dot(piece[:, columns], precond_ref[k], preferred_element_type=jnp.float32)
            rounded_ref[:rows, columns] = value.astype(jnp.bfloat16)
            value = value * value
            squares += value[:, :128] + value[:, 128:]
        starts = [first_row(place, core, *block, part) for block in blocks for part in range(4)]
        for n, start in enumerate(starts):
            sums_ref[pl.ds(start, SHARD), :] = squares[n * SHARD : (n + 1) * SHARD]
        for k in range(4):
            value = jnp.dot(rounded_ref[:rows, :], turned_ref[k], preferred_element_type=jnp.float32)
            columns = slice((k % 2) * 256, (k % 2 + 1) * 256)
            for n, start in enumerate(starts):
                part = value[n * SHARD : (n + 1) * SHARD]
                if k < 2:
                    keep_ref[pl.ds(start, SHARD), columns] = part
                else:
                    send_ref[pl.ds(start, SHARD), columns] = part.astype(jnp.bfloat16)


def pack_kernel(sums_ref, train_ref, lanes_ref, rows_ref):
    lanes_ref[...] = jnp.sum(sums_ref[...].T, axis=0, keepdims=True)
    rows = []
    for j in range(2):
        rows += split3(lanes_ref[:, j * 512 : (j + 1) * 512])
    rows += split3(jnp.concatenate([train_ref[2:3, :], train_ref[3:4, :]], axis=1))
    rows.append(jnp.zeros((SHARD - len(rows), 512), jnp.bfloat16))
    rows_ref[...] = jnp.concatenate(rows, axis=0)


def join3(ref, base, row):
    return sum(ref[base + row + i : base + row + i + 1, :].astype(jnp.float32) for i in range(3))


def chip_kernel(keep_ref, got_ref, lanes_ref, train_ref, mine_ref, send_ref, lanes2_ref, train2_ref):
    rows = keep_ref.shape[0]
    mine_ref[...] = keep_ref[:, :256] + got_ref[:rows, :256].astype(jnp.float32)
    theirs = keep_ref[:, 256:] + got_ref[:rows, 256:].astype(jnp.float32)
    send_ref[:rows, :] = theirs.astype(jnp.bfloat16)
    got = got_ref[rows:, :].astype(jnp.float32)
    extra = []
    for j in range(2):
        total = lanes_ref[:, j * 512 : (j + 1) * 512] + (got[3 * j : 3 * j + 1] + got[3 * j + 1 : 3 * j + 2] + got[3 * j + 2 : 3 * j + 3])
        lanes2_ref[:, j * 512 : (j + 1) * 512] = total
        extra += split3(total[:, :256]) + split3(total[:, 256:])
    train = got[6:7] + got[7:8] + got[8:9]
    train2_ref[...] = train_ref[0:1, :] + train[:, :256]
    extra += split3(train_ref[1:2, :] + train[:, 256:])
    extra.append(jnp.zeros((SHARD - len(extra), 256), jnp.bfloat16))
    send_ref[rows:, :] = jnp.concatenate(extra, axis=0)


def finish_kernel(mine_ref, got_ref, lanes_ref, train_ref, out_ref):
    rows = mine_ref.shape[0]
    got = got_ref[rows:, :].astype(jnp.float32)
    sums = [got[3 * j : 3 * j + 1] + got[3 * j + 1 : 3 * j + 2] + got[3 * j + 2 : 3 * j + 3] for j in range(5)]
    query = lanes_ref[...] + jnp.concatenate(sums[:4], axis=1)
    query = 1.0 / jnp.sqrt(query + EPS)
    query = jnp.broadcast_to(query, (128, rows)).T
    train = (1.0 / jnp.sqrt(train_ref[...] + sums[4] + EPS)) * math.sqrt(F)
    for j in range(2):
        columns = slice(j * 128, (j + 1) * 128)
        total = mine_ref[:, columns] + got_ref[:rows, columns].astype(jnp.float32)
        out_ref[:, columns] = total * query * train[:, columns]


def call(kernel, outs, inputs, scratch=(), flops=0, moved=0, smem=0):
    return pl.pallas_call(
        kernel,
        out_shape=[jax.ShapeDtypeStruct(s, d) for s, d in outs],
        in_specs=[SMEM] * smem + [VMEM] * (len(inputs) - smem),
        out_specs=[VMEM] * len(outs),
        scratch_shapes=list(scratch),
        compiler_params=pltpu.CompilerParams(vmem_limit_bytes=24 * MIB),
        cost_estimate=pl.CostEstimate(flops=flops, bytes_accessed=moved, transcendentals=0),
    )(*inputs)


def on_device(query_grads, train_grads, precond):
    f32, bf16 = jnp.float32, jnp.bfloat16
    row = lax.axis_index("rows")
    place = jnp.stack([row // (NY * NX), row // NX % NY, row % NX, lax.axis_index("feat")]).astype(jnp.int32)
    turned, train_sums = call(
        prepare_kernel,
        [((4, 2048, 256), bf16), ((4, 256), f32)],
        [place, train_grads],
        moved=8 * MIB,
        smem=1,
    )
    pieces = gather(query_grads)
    keep, send, squares = call(
        products_kernel,
        [((1024, 512), f32), ((1024, 512), bf16), ((1024, 128), f32)],
        [place, turned, precond, *pieces],
        scratch=[pltpu.VMEM((256, 2048), bf16)],
        flops=5 << 30,
        smem=1,
    )
    lanes, extra = call(pack_kernel, [((1, 1024), f32), ((SHARD, 512), bf16)], [squares, train_sums])
    got = across(join(send, extra), 1)
    mine, send, lanes, train = call(
        chip_kernel,
        [((1024, 256), f32), ((1024 + SHARD, 256), bf16), ((1, 1024), f32), ((1, 256), f32)],
        [keep, got, lanes, train_sums],
    )
    got = across(send, 2)
    return call(finish_kernel, [((1024, 256), f32)], [mine, got, lanes, train])[0]


def solution(mesh):
    in_specs = (P("rows", "feat"), P("rows", "feat"), P("feat", None, None))
    out_specs = P(None, ("rows", "feat"))
    return jax.shard_map(
        on_device, mesh=mesh, in_specs=in_specs, out_specs=out_specs, check_vma=False
    )
```

```python
import math

import jax
import jax.numpy as jnp
from jax import lax
from jax.experimental import pallas as pl
from jax.experimental.pallas import tpu as pltpu
from jax.sharding import PartitionSpec as P

F = 8192
EPS = 1e-06
NZ, NY, NX = 8, 4, 2
SHARD = 16
BLOCK = 4 * SHARD
NEAR = (0, -1, 1, -2)
VMEM = pl.BlockSpec(memory_space=pltpu.VMEM)
SMEM = pl.BlockSpec(memory_space=pltpu.SMEM)
MIB = 1 << 20


def row_index(z, y, x):
    return (z % NZ) * (NY * NX) + (y % NY) * NX + x % NX


def shift(value, even, odd=None):
    odd = even if odd is None else odd
    pairs = []
    for z in range(NZ):
        for y in range(NY):
            for x in range(NX):
                for f in range(4):
                    dz, dy, dx = odd if f % 2 else even
                    there = row_index(z + dz, y + dy, x + dx)
                    pairs.append((row_index(z, y, x) * 4 + f, there * 4 + f))
    return lax.ppermute(value, ("rows", "feat"), pairs)


def across(value, mask):
    return lax.ppermute(value, "feat", [(f, f ^ mask) for f in range(4)])


def join(*parts):
    return jnp.concatenate(parts, axis=0)


def together(*values):
    return lax.optimization_barrier(values)


def gather(own, early, first_product):
    pair = join(own, shift(own, (4, 0, 0)))
    four = join(pair, shift(pair, (0, 0, 1)))
    first = [
        shift(four, (0, 1, 0), (1, 0, 0)),
        shift(four, (0, -1, 0), (-1, 0, 0)),
        shift(four, (0, 2, 0), (2, 0, 0)),
    ]
    prepared = early(four)
    low, high, *prepared = together(join(four, first[0]), join(*first[1:]), *prepared)
    up, down = (1, 0, 0), (0, 1, 0)
    back_up, back_down = (-1, 0, 0), (0, -1, 0)
    low_before, high_after = shift(low, up, down), shift(high, back_up, back_down)
    high_before, low_after = shift(high, up, down), shift(low, back_up, back_down)
    product = first_product((low, high), prepared)
    low_before, high_after, *product = together(low_before, high_after, *product)
    low_far, high_far = shift(low_before, up, down), shift(high_after, back_up, back_down)
    return prepared, product, (low_before, high_after), (high_before, low_after), (low_far, high_far)


LOW, HIGH = NEAR[:2], NEAR[2:]
STAGES = (
    [[(a, 0) for a in LOW], [(a, 0) for a in HIGH]],
    [[(a, -1) for a in LOW], [(a, 1) for a in HIGH]],
    [[(a, -1) for a in HIGH], [(a, 1) for a in LOW]],
    [[(a, -2) for a in LOW], [(a, 2) for a in HIGH]],
)
ORDER = [block for stage in STAGES for piece in stage for block in piece]
STAGE_ROWS = [sum(len(piece) for piece in stage) * BLOCK for stage in STAGES]


def wrap(step):
    return -2 if step == 2 else step


EARLY = [block for block in ORDER if 2 not in map(abs, block)]
LATE = [block for block in ORDER if 2 in map(abs, block)]


def slot(block):
    at = ORDER.index(block) * BLOCK
    for stage, rows in enumerate(STAGE_ROWS):
        if at < rows:
            return stage, at
        at -= rows


def twin(block):
    other = (wrap(block[1]), wrap(block[0]))
    return next(b for b in ORDER if (wrap(b[0]), wrap(b[1])) == other)


def depth(core, block):
    return jnp.where(core == 0, block[1], block[0])


def first_row(place, block, part):
    z, y, x, core = place[0], place[1], place[2], place[3] % 2
    dz = depth(core, block)
    dy = jnp.where(core == 0, block[0], block[1])
    zz = lax.rem(z + dz + (4 * (part % 2) + NZ), NZ)
    yy = lax.rem(y + dy + NY, NY)
    xx = lax.rem(x + part // 2, NX)
    return pl.multiple_of((zz * (NY * NX) + yy * NX + xx) * SHARD, SHARD)


def twin_row(place, block, part):
    core = place[3] % 2
    other = twin(block)
    away = lax.rem(depth(core, block) - depth(1 - core, other) + 8, 8) // 4
    start = slot(other)[1]
    if slot(other)[0] == len(STAGES) - 1:
        start = start % (STAGE_ROWS[-1] // 2)
    return pl.multiple_of(start + (part // 2) * 2 * SHARD + ((part % 2) ^ away) * SHARD, SHARD)


def split3(value):
    high = value.astype(jnp.bfloat16)
    rest = value - high.astype(jnp.float32)
    middle = rest.astype(jnp.bfloat16)
    low = (rest - middle.astype(jnp.float32)).astype(jnp.bfloat16)
    return [high, middle, low]


def prepare_kernel(place, train_ref, turned_ref, sums_ref):
    me = place[3]
    for k, mask in enumerate((0, 2, 1, 3)):
        start = pl.multiple_of((me ^ mask) * 256, 256)
        for j in range(0, 2048, 512):
            block = train_ref[pl.ds(start, 256), j : j + 512].T
            turned_ref[k, j : j + 512, :] = block
            wide = block.astype(jnp.float32)
            part = jnp.sum(wide * wide, axis=0, keepdims=True)
            if j == 0:
                sums_ref[k : k + 1, :] = part
            else:
                sums_ref[k : k + 1, :] += part


def products(pieces, turned_ref, precond_ref, keep_ref, send_refs, sums_ref, rounded_ref):
    base = 0
    for piece in pieces:
        rows = piece.shape[0]
        here = slice(base, base + rows)
        squares = jnp.zeros((rows, 128), jnp.float32)
        for k in range(8):
            columns = slice(k * 256, (k + 1) * 256)
            value = jnp.dot(piece[:, columns], precond_ref[k], preferred_element_type=jnp.float32)
            rounded_ref[here, columns] = value.astype(jnp.bfloat16)
            value = value * value
            squares += value[:, :128] + value[:, 128:]
        sums_ref[here, :] = squares
        base += rows
    for base in range(0, base, 256):
        here = slice(base, base + 256)
        for k in (2, 3, 0, 1):
            value = jnp.dot(rounded_ref[here, :], turned_ref[k], preferred_element_type=jnp.float32)
            columns = slice((k % 2) * 256, (k % 2 + 1) * 256)
            if k < 2:
                keep_ref[here, columns] = value
            else:
                value = value.astype(jnp.bfloat16)
                rows = 256 // len(send_refs)
                for n, send_ref in enumerate(send_refs):
                    send_ref[slice(base, base + rows), columns] = value[n * rows : (n + 1) * rows]


def products_kernel(turned_ref, precond_ref, *refs):
    keep_ref, send_ref, sums_ref, rounded_ref = refs[-4:]
    products(refs[:-4], turned_ref, precond_ref, keep_ref, [send_ref], sums_ref, rounded_ref)


def last_products_kernel(
    place, turned_ref, precond_ref, low, high, sums0, sums1, sums2, train_ref, keep_ref, send_low, send_high, lanes_ref, rounded_ref, sums3, all_sums
):
    products((low, high), turned_ref, precond_ref, keep_ref, [send_low, send_high], sums3, rounded_ref)
    sums = (sums0, sums1, sums2, sums3)
    for block in ORDER:
        stage, at = slot(block)
        for part in range(4):
            here = slice(at + part * SHARD, at + (part + 1) * SHARD)
            all_sums[pl.ds(first_row(place, block, part), SHARD), :] = sums[stage][here, :]
    lanes = jnp.sum(all_sums[...].T, axis=0, keepdims=True)
    lanes_ref[...] = lanes
    extra = split3(lanes[:, :512]) + split3(lanes[:, 512:])
    extra += split3(jnp.concatenate([train_ref[2:3, :], train_ref[3:4, :]], axis=1))
    extra.append(jnp.zeros((SHARD - len(extra), 512), jnp.bfloat16))
    send_high[low.shape[0] :, :] = jnp.concatenate(extra, axis=0)


def add_blocks(place, blocks, keeps, gots, mine_ref, send_ref, at=0):
    first = at
    for block in blocks:
        stage, base = slot(block)
        there, start = slot(twin(block))
        if there == len(STAGES) - 1 and start >= STAGE_ROWS[-1] // 2:
            there += 1
        for part in range(4):
            own = keeps[stage][base + part * SHARD : base + (part + 1) * SHARD, :]
            total = own + gots[there][pl.ds(twin_row(place, block, part), SHARD), :].astype(jnp.float32)
            mine_ref[at : at + SHARD, :] = total[:, :256]
            send_ref[at - first : at - first + SHARD, :] = total[:, 256:].astype(jnp.bfloat16)
            at += SHARD


def early_kernel(place, keep0, keep1, keep2, got0, got1, got2, mine_ref, send_ref):
    add_blocks(place, EARLY, (keep0, keep1, keep2), (got0, got1, got2), mine_ref, send_ref)


def late_kernel(place, *refs):
    keeps, gots, rest = refs[: len(STAGES)], refs[len(STAGES) : 2 * len(STAGES) + 1], refs[2 * len(STAGES) + 1 :]
    lanes_ref, train_ref, mine_ref, send_low, send_high, lanes2_ref, train2_ref = rest
    add_blocks(place, LATE[:4], keeps, gots, mine_ref, send_low)
    add_blocks(place, LATE[4:], keeps, gots, mine_ref, send_high, 4 * BLOCK)
    got = gots[-1][keeps[-1].shape[0] // 2 :, :].astype(jnp.float32)
    extra = []
    for j in range(2):
        columns = slice(j * 512, (j + 1) * 512)
        total = lanes_ref[:, columns] + sum3(got, 3 * j)
        lanes2_ref[:, columns] = total
        extra += split3(total[:, :256]) + split3(total[:, 256:])
    train = sum3(got, 6)
    train2_ref[...] = train_ref[0:1, :] + train[:, :256]
    extra += split3(train_ref[1:2, :] + train[:, 256:])
    extra.append(jnp.zeros((SHARD - len(extra), 256), jnp.bfloat16))
    send_high[len(LATE[4:]) * BLOCK :, :] = jnp.concatenate(extra, axis=0)


def sum3(rows, at):
    return rows[at : at + 1] + (rows[at + 1 : at + 2] + rows[at + 2 : at + 3])


def merge_kernel(place, mine0, got0, mine1, all_ref):
    for blocks, mine, other in ((EARLY, mine0, got0), (LATE, mine1, None)):
        at = 0
        for block in blocks:
            for part in range(4):
                total = mine[at : at + SHARD, :]
                if other is not None:
                    total = total + other[at : at + SHARD, :].astype(jnp.float32)
                all_ref[pl.ds(first_row(place, block, part), SHARD), :] = total
                at += SHARD


def finish_kernel(place, all_ref, got1, got2, lanes_ref, train_ref, out_ref, sums_ref):
    sums_ref[...] = all_ref[...]
    for blocks, got in ((LATE[:4], got1), (LATE[4:], got2)):
        at = 0
        for block in blocks:
            for part in range(4):
                rows = pl.ds(first_row(place, block, part), SHARD)
                sums_ref[rows, :] += got[at : at + SHARD, :].astype(jnp.float32)
                at += SHARD
    got = got2[at:, :].astype(jnp.float32)
    query = lanes_ref[...] + jnp.concatenate([sum3(got, 3 * j) for j in range(4)], axis=1)
    query = 1.0 / jnp.sqrt(query + EPS)
    train = (1.0 / jnp.sqrt(train_ref[...] + sum3(got, 12) + EPS)) * math.sqrt(F)
    for i in range(0, 1024, 128):
        rows = slice(i, i + 128)
        scale = jnp.broadcast_to(query[:, rows], (128, 128)).T
        for j in range(0, 256, 128):
            columns = slice(j, j + 128)
            out_ref[rows, columns] = sums_ref[rows, columns] * scale * train[:, columns]


def call(kernel, outs, inputs, scratch=(), smem=0, moved=1):
    return pl.pallas_call(
        kernel,
        out_shape=[jax.ShapeDtypeStruct(s, d) for s, d in outs],
        in_specs=[SMEM] * smem + [VMEM] * (len(inputs) - smem),
        out_specs=[VMEM] * len(outs),
        scratch_shapes=list(scratch),
        compiler_params=pltpu.CompilerParams(vmem_limit_bytes=24 * MIB),
        cost_estimate=pl.CostEstimate(flops=1, bytes_accessed=moved, transcendentals=0),
    )(*inputs)


def on_device(query_grads, train_grads, precond):
    f32, bf16 = jnp.float32, jnp.bfloat16
    row = lax.axis_index("rows")
    place = jnp.stack([row // (NY * NX), row // NX % NY, row % NX, lax.axis_index("feat")]).astype(jnp.int32)

    def prepare(four):
        train, _ = together(train_grads, four)
        return call(
            prepare_kernel,
            [((4, 2048, 256), bf16), ((4, 256), f32)],
            [place, train],
            smem=1,
        )

    def product(pieces, prepared):
        rows = sum(piece.shape[0] for piece in pieces)
        return call(
            products_kernel,
            [((rows, 512), f32), ((rows, 512), bf16), ((rows, 128), f32)],
            [prepared[0], precond, *pieces],
            scratch=[pltpu.VMEM((rows, 2048), bf16)],
        )

    prepared, done, *stages, last = gather(query_grads, prepare, product)
    turned, train_sums = prepared
    keep, send, squares = done
    keeps, gots, sums = [keep], [across(send, 1)], [squares]
    for pieces in stages:
        *pieces, _ = together(*pieces, send)
        keep, send, squares = product(pieces, prepared)
        keeps.append(keep)
        gots.append(across(send, 1))
        sums.append(squares)
    early = len(EARLY) * BLOCK
    late = len(LATE) * BLOCK
    mine0, send = call(
        early_kernel, [((early, 256), f32), ((early, 256), bf16)], [place, *keeps, *gots], smem=1
    )
    got0 = across(send, 2)
    low, high, _ = together(*last, send)
    rows = STAGE_ROWS[-1]
    keep, send_low, send_high, lanes = call(
        last_products_kernel,
        [((rows, 512), f32), ((rows // 2, 512), bf16), ((rows // 2 + SHARD, 512), bf16), ((1, 1024), f32)],
        [place, turned, precond, low, high, *sums, train_sums],
        scratch=[pltpu.VMEM((rows, 2048), bf16), pltpu.VMEM((rows, 128), f32), pltpu.VMEM((1024, 128), f32)],
        smem=1,
    )
    mine1, send_low, send_high, lanes, train = call(
        late_kernel,
        [
            ((late, 256), f32),
            ((4 * BLOCK, 256), bf16),
            ((late - 4 * BLOCK + SHARD, 256), bf16),
            ((1, 1024), f32),
            ((1, 256), f32),
        ],
        [place, *keeps, keep, *gots, across(send_low, 1), across(send_high, 1), lanes, train_sums],
        smem=1,
    )
    got1, got2 = across(send_low, 2), across(send_high, 2)
    merged = call(merge_kernel, [((1024, 256), f32)], [place, mine0, got0, mine1], smem=1)[0]
    return call(
        finish_kernel,
        [((1024, 256), f32)],
        [place, merged, got1, got2, lanes, train],
        scratch=[pltpu.VMEM((1024, 256), f32)],
        smem=1,
    )[0]


def solution(mesh):
    in_specs = (P("rows", "feat"), P("rows", "feat"), P("feat", None, None))
    out_specs = P(None, ("rows", "feat"))
    return jax.shard_map(
        on_device, mesh=mesh, in_specs=in_specs, out_specs=out_specs, check_vma=False
    )
```

```python
import math

import jax
import jax.numpy as jnp
from jax import lax
from jax.experimental import pallas as pl
from jax.experimental.pallas import tpu as pltpu
from jax.sharding import PartitionSpec as P

F = 8192
EPS = 1e-06
NZ, NY, NX = 8, 4, 2
SHARD = 16
BLOCK = 4 * SHARD
NEAR = (0, -1, 1, -2)
VMEM = pl.BlockSpec(memory_space=pltpu.VMEM)
SMEM = pl.BlockSpec(memory_space=pltpu.SMEM)
MIB = 1 << 20


def row_index(z, y, x):
    return (z % NZ) * (NY * NX) + (y % NY) * NX + x % NX


def shift(value, even, odd=None):
    odd = even if odd is None else odd
    pairs = []
    for z in range(NZ):
        for y in range(NY):
            for x in range(NX):
                for f in range(4):
                    dz, dy, dx = odd if f % 2 else even
                    there = row_index(z + dz, y + dy, x + dx)
                    pairs.append((row_index(z, y, x) * 4 + f, there * 4 + f))
    return lax.ppermute(value, ("rows", "feat"), pairs)


def across(value, mask):
    return lax.ppermute(value, "feat", [(f, f ^ mask) for f in range(4)])


def join(*parts):
    return jnp.concatenate(parts, axis=0)


def together(*values):
    return lax.optimization_barrier(values)


def gather(own, early, first_product):
    near = call(copy_kernel, [(own.shape, own.dtype)], [own])[0]
    pair = join(near, shift(own, (4, 0, 0)))
    four = join(pair, shift(pair, (0, 0, 1)))
    first = [
        shift(four, (0, 1, 0), (1, 0, 0)),
        shift(four, (0, -1, 0), (-1, 0, 0)),
        shift(four, (0, 2, 0), (2, 0, 0)),
    ]
    prepared = early(four)
    low, high, *prepared = together(join(four, first[0]), join(*first[1:]), *prepared)
    up, down = (1, 0, 0), (0, 1, 0)
    back_up, back_down = (-1, 0, 0), (0, -1, 0)
    low_before, high_after = shift(low, up, down), shift(high, back_up, back_down)
    high_before, low_after = shift(high, up, down), shift(low, back_up, back_down)
    product = first_product((low, high), prepared)
    low_before, high_after, *product = together(low_before, high_after, *product)
    low_far, high_far = shift(low_before, up, down), shift(high_after, back_up, back_down)
    return prepared, product, (low_before, high_after), (high_before, low_after), (low_far, high_far)


LOW, HIGH = NEAR[:2], NEAR[2:]
STAGES = (
    [[(a, 0) for a in LOW], [(a, 0) for a in HIGH]],
    [[(a, -1) for a in LOW], [(a, 1) for a in HIGH]],
    [[(a, -1) for a in HIGH], [(a, 1) for a in LOW]],
    [[(a, -2) for a in LOW], [(a, 2) for a in HIGH]],
)
ORDER = [block for stage in STAGES for piece in stage for block in piece]
STAGE_ROWS = [sum(len(piece) for piece in stage) * BLOCK for stage in STAGES]
SENDS = (1, 1, 2, 2)


def wrap(step):
    return -2 if step == 2 else step


EARLY = [block for block in ORDER if 2 not in map(abs, block)]
LATE = [block for block in ORDER if 2 in map(abs, block)]


def slot(block):
    at = ORDER.index(block) * BLOCK
    for stage, rows in enumerate(STAGE_ROWS):
        if at < rows:
            return stage, at
        at -= rows


def twin(block):
    other = (wrap(block[1]), wrap(block[0]))
    return next(b for b in ORDER if (wrap(b[0]), wrap(b[1])) == other)


def depth(core, block):
    return block[1] if block[0] == block[1] else jnp.where(core == 0, block[1], block[0])


def first_rows(place, block):
    z, y, x, core = place[0], place[1], place[2], place[3] & 1
    dz = depth(core, block)
    dy = depth(1 - core, block)
    row = ((z + dz) & (NZ - 1)) * (NY * NX) + ((y + dy) & (NY - 1)) * NX + x
    return [pl.multiple_of((row ^ (NZ // 2 * NY * NX * (part % 2) + part // 2)) * SHARD, SHARD) for part in range(4)]


def twin_rows(place, block):
    core = place[3] & 1
    stage, start = slot(twin(block))
    each = STAGE_ROWS[stage] // SENDS[stage]
    parts = [start % each + part * SHARD for part in range(4)]
    if 2 in (block[1], twin(block)[1]):
        away = (((depth(core, block) - depth(1 - core, twin(block))) >> 2) & 1) * SHARD
        parts = [pl.multiple_of(row ^ away, SHARD) for row in parts]
    return sum(SENDS[:stage]) + start // each, parts


def split3(value):
    high = value.astype(jnp.bfloat16)
    rest = value - high.astype(jnp.float32)
    middle = rest.astype(jnp.bfloat16)
    low = (rest - middle.astype(jnp.float32)).astype(jnp.bfloat16)
    return [high, middle, low]


def copy_kernel(from_ref, to_ref):
    to_ref[...] = from_ref[...]


def prepare_kernel(place, train_ref, turned_ref, sums_ref):
    me = place[3]
    for k, mask in enumerate((0, 2, 1, 3)):
        start = pl.multiple_of((me ^ mask) * 256, 256)
        for j in range(0, 2048, 512):
            block = train_ref[pl.ds(start, 256), j : j + 512].T
            turned_ref[k, j : j + 512, :] = block
            wide = block.astype(jnp.float32)
            part = jnp.sum(wide * wide, axis=0, keepdims=True)
            if j == 0:
                sums_ref[k : k + 1, :] = part
            else:
                sums_ref[k : k + 1, :] += part


def condition(pieces, precond_ref, sums_ref, rounded_ref):
    base = 0
    for piece in pieces:
        rows = piece.shape[0]
        here = slice(base, base + rows)
        squares = jnp.zeros((rows, 128), jnp.float32)
        for k in range(8):
            columns = slice(k * 256, (k + 1) * 256)
            value = jnp.dot(piece[:, columns], precond_ref[k], preferred_element_type=jnp.float32)
            rounded_ref[here, columns] = value.astype(jnp.bfloat16)
            value = value * value
            squares += value[:, :128] + value[:, 128:]
        sums_ref[here, :] = squares
        base += rows


def multiply(rounded_ref, turned_ref, refs, first):
    each = rounded_ref.shape[0] // len(refs)
    for k in range(2):
        value = jnp.dot(rounded_ref[...], turned_ref[first + k], preferred_element_type=jnp.float32)
        for n, ref in enumerate(refs):
            ref[:each, k * 256 : (k + 1) * 256] = value[n * each : (n + 1) * each].astype(ref.dtype)


def products_kernel(turned_ref, precond_ref, low, high, keep_ref, *refs):
    *send_refs, sums_ref, rounded_ref = refs
    condition((low, high), precond_ref, sums_ref, rounded_ref)
    multiply(rounded_ref, turned_ref, send_refs, 2)
    multiply(rounded_ref, turned_ref, [keep_ref], 0)


def last_kept_kernel(turned_ref, rounded_ref, keep_ref):
    multiply(rounded_ref, turned_ref, [keep_ref], 0)


def last_sent_kernel(
    place, turned_ref, precond_ref, low, high, sums0, sums1, sums2, train_ref, rounded_ref, send_low, send_high, lanes_ref, sums3, all_sums
):
    condition((low, high), precond_ref, sums3, rounded_ref)
    multiply(rounded_ref, turned_ref, [send_low, send_high], 2)
    sums = (sums0, sums1, sums2, sums3)
    for block in ORDER:
        stage, at = slot(block)
        for part, row in enumerate(first_rows(place, block)):
            here = slice(at + part * SHARD, at + (part + 1) * SHARD)
            all_sums[pl.ds(row, SHARD), :] = sums[stage][here, :]
    lanes = jnp.sum(all_sums[...].T, axis=0, keepdims=True)
    lanes_ref[...] = lanes
    extra = split3(lanes[:, :512]) + split3(lanes[:, 512:])
    extra += split3(jnp.concatenate([train_ref[2:3, :], train_ref[3:4, :]], axis=1))
    extra.append(jnp.zeros((SHARD - len(extra), 512), jnp.bfloat16))
    send_high[low.shape[0] :, :] = jnp.concatenate(extra, axis=0)


def add_blocks(place, blocks, keeps, gots, mine_ref, send_ref, at=0):
    first = at
    for block in blocks:
        stage, base = slot(block)
        there, rows = twin_rows(place, block)
        for part, row in enumerate(rows):
            own = keeps[stage][base + part * SHARD : base + (part + 1) * SHARD, :]
            total = own + gots[there][pl.ds(row, SHARD), :].astype(jnp.float32)
            mine_ref[at : at + SHARD, :] = total[:, :256]
            send_ref[at - first : at - first + SHARD, :] = total[:, 256:].astype(jnp.bfloat16)
            at += SHARD


def early_kernel(place, *refs):
    keeps, gots = refs[: len(STAGES) - 1], refs[len(STAGES) - 1 : -2]
    add_blocks(place, EARLY, keeps, gots, *refs[-2:])


def late_kernel(place, *refs):
    first, last = len(STAGES), len(STAGES) + sum(SENDS)
    keeps, gots, rest = refs[:first], refs[first:last], refs[last:]
    lanes_ref, train_ref, mine_ref, send_low, send_high, lanes2_ref, train2_ref = rest
    add_blocks(place, LATE[:4], keeps, gots, mine_ref, send_low)
    add_blocks(place, LATE[4:], keeps, gots, mine_ref, send_high, 4 * BLOCK)
    got = gots[-1][keeps[-1].shape[0] // 2 :, :].astype(jnp.float32)
    extra = []
    for j in range(2):
        columns = slice(j * 512, (j + 1) * 512)
        total = lanes_ref[:, columns] + sum3(got, 3 * j)
        lanes2_ref[:, columns] = total
        extra += split3(total[:, :256]) + split3(total[:, 256:])
    train = sum3(got, 6)
    train2_ref[...] = train_ref[0:1, :] + train[:, :256]
    extra += split3(train_ref[1:2, :] + train[:, 256:])
    extra.append(jnp.zeros((SHARD - len(extra), 256), jnp.bfloat16))
    send_high[len(LATE[4:]) * BLOCK :, :] = jnp.concatenate(extra, axis=0)


def sum3(rows, at):
    return rows[at : at + 1] + (rows[at + 1 : at + 2] + rows[at + 2 : at + 3])


def merge_kernel(mine0, got0, all_ref):
    all_ref[...] = mine0[...] + got0[...].astype(jnp.float32)


def finish_kernel(place, early_ref, mine1, got1, got2, lanes_ref, train_ref, out_ref, scale_ref, sums_ref, sem):
    split = got1.shape[0]
    late = mine1.shape[0]
    got = got2[late - split :, :].astype(jnp.float32)
    query = lanes_ref[...] + jnp.concatenate([sum3(got, 3 * j) for j in range(4)], axis=1)
    query = 1.0 / jnp.sqrt(query + EPS)
    for i in range(0, 1024, 128):
        scale_ref[i : i + 128, :] = jnp.broadcast_to(query[:, i : i + 128], (128, 128)).T
    train = (1.0 / jnp.sqrt(train_ref[...] + sum3(got, 12) + EPS)) * math.sqrt(F)
    at = 0
    for block in EARLY + LATE:
        for row in first_rows(place, block):
            base = at - len(EARLY) * BLOCK
            if base < 0:
                total = early_ref[at : at + SHARD, :]
            else:
                other = got1[base : base + SHARD, :] if base < split else got2[base - split : base - split + SHARD, :]
                total = mine1[base : base + SHARD, :] + other.astype(jnp.float32)
            rows = pl.ds(row, SHARD)
            scale = scale_ref[rows, :]
            for j in range(0, 256, 128):
                sums_ref[at : at + SHARD, j : j + 128] = total[:, j : j + 128] * scale * train[:, j : j + 128]
            pltpu.make_async_copy(sums_ref.at[at : at + SHARD, :], out_ref.at[rows, :], sem).start()
            at += SHARD
    pltpu.make_async_copy(sums_ref, out_ref, sem).wait()


def call(kernel, outs, inputs, scratch=(), smem=0, out_spec=VMEM):
    return pl.pallas_call(
        kernel,
        out_shape=[jax.ShapeDtypeStruct(s, d) for s, d in outs],
        in_specs=[SMEM] * smem + [VMEM] * (len(inputs) - smem),
        out_specs=[out_spec] * len(outs),
        scratch_shapes=list(scratch),
        compiler_params=pltpu.CompilerParams(vmem_limit_bytes=24 * MIB),
        cost_estimate=pl.CostEstimate(flops=1, bytes_accessed=1, transcendentals=0),
    )(*inputs)


def on_device(query_grads, train_grads, precond):
    f32, bf16 = jnp.float32, jnp.bfloat16
    row = lax.axis_index("rows")
    place = jnp.stack([row // (NY * NX), row // NX % NY, row % NX, lax.axis_index("feat")]).astype(jnp.int32)

    def prepare(four):
        train, _ = together(train_grads, four)
        return call(
            prepare_kernel,
            [((4, 2048, 256), bf16), ((4, 256), f32)],
            [place, train],
            smem=1,
        )

    def product(pieces, prepared, sends=1):
        rows = sum(piece.shape[0] for piece in pieces)
        return call(
            products_kernel,
            [((rows, 512), f32), *[((rows // sends, 512), bf16)] * sends, ((rows, 128), f32)],
            [prepared[0], precond, *pieces],
            scratch=[pltpu.VMEM((rows, 2048), bf16)],
        )

    prepared, done, *stages, last = gather(query_grads, prepare, product)
    turned, train_sums = prepared
    keep, send, squares = done
    keeps, gots, sums = [keep], [across(send, 1)], [squares]
    for n, pieces in enumerate(stages):
        *pieces, _ = together(*pieces, gots[-1] if n else send)
        keep, *sends, squares = product(pieces, prepared, SENDS[n + 1])
        keeps.append(keep)
        gots += [across(send, 1) for send in sends]
        sums.append(squares)
    early = len(EARLY) * BLOCK
    late = len(LATE) * BLOCK
    mine0, send = call(
        early_kernel, [((early, 256), f32), ((early, 256), bf16)], [place, *keeps, *gots], smem=1
    )
    got0 = across(send, 2)
    low, high, _ = together(*last, send)
    rows = STAGE_ROWS[-1]
    rounded, send_low, send_high, lanes = call(
        last_sent_kernel,
        [((rows, 2048), bf16), ((rows // 2, 512), bf16), ((rows // 2 + SHARD, 512), bf16), ((1, 1024), f32)],
        [place, turned, precond, low, high, *sums, train_sums],
        scratch=[pltpu.VMEM((rows, 128), f32), pltpu.VMEM((1024, 128), f32)],
        smem=1,
    )
    keep = call(last_kept_kernel, [((rows, 512), f32)], [turned, rounded])[0]
    mine1, send_low, send_high, lanes, train = call(
        late_kernel,
        [
            ((late, 256), f32),
            ((4 * BLOCK, 256), bf16),
            ((late - 4 * BLOCK + SHARD, 256), bf16),
            ((1, 1024), f32),
            ((1, 256), f32),
        ],
        [place, *keeps, keep, *gots, across(send_low, 1), across(send_high, 1), lanes, train_sums],
        smem=1,
    )
    got1, got2 = across(send_low, 2), across(send_high, 2)
    merged = call(merge_kernel, [((early, 256), f32)], [mine0, got0])[0]
    return call(
        finish_kernel,
        [((1024, 256), f32)],
        [place, merged, mine1, got1, got2, lanes, train],
        scratch=[pltpu.VMEM((1024, 128), f32), pltpu.VMEM((1024, 256), f32), pltpu.SemaphoreType.DMA],
        smem=1,
        out_spec=pl.BlockSpec(memory_space=pl.ANY),
    )[0]


def solution(mesh):
    in_specs = (P("rows", "feat"), P("rows", "feat"), P("feat", None, None))
    out_specs = P(None, ("rows", "feat"))
    return jax.shard_map(
        on_device, mesh=mesh, in_specs=in_specs, out_specs=out_specs, check_vma=False
    )
```

```python
import math

import jax
import jax.numpy as jnp
from jax import lax
from jax.experimental import pallas as pl
from jax.experimental.pallas import tpu as pltpu
from jax.sharding import PartitionSpec as P

F = 8192
EPS = 1e-06
NZ, NY, NX = 8, 4, 2
SHARD = 16
BLOCK = 4 * SHARD
NEAR = (0, -1, 1, -2)
VMEM = pl.BlockSpec(memory_space=pltpu.VMEM)
MIB = 1 << 20


def row_index(z, y, x):
    return (z % NZ) * (NY * NX) + (y % NY) * NX + x % NX


def shift(value, even, odd=None):
    odd = even if odd is None else odd
    pairs = []
    for z in range(NZ):
        for y in range(NY):
            for x in range(NX):
                for f in range(4):
                    dz, dy, dx = odd if f % 2 else even
                    there = row_index(z + dz, y + dy, x + dx)
                    pairs.append((row_index(z, y, x) * 4 + f, there * 4 + f))
    return lax.ppermute(value, ("rows", "feat"), pairs)


def across(value, mask):
    return lax.ppermute(value, "feat", [(f, f ^ mask) for f in range(4)])


def join(*parts):
    return jnp.concatenate(parts, axis=0)


def together(*values):
    return lax.optimization_barrier(values)


def gather(own, early, first_product):
    near = call(copy_kernel, [(own.shape, own.dtype)], [own])[0]
    pair = join(near, shift(own, (4, 0, 0)))
    four = join(pair, shift(pair, (0, 0, 1)))
    first = [
        shift(four, (0, 1, 0), (1, 0, 0)),
        shift(four, (0, -1, 0), (-1, 0, 0)),
        shift(four, (0, 2, 0), (2, 0, 0)),
    ]
    prepared = early(four)
    low, high, *prepared = together(join(four, first[0]), join(*first[1:]), *prepared)
    up, down = (1, 0, 0), (0, 1, 0)
    back_up, back_down = (-1, 0, 0), (0, -1, 0)
    low_before, high_after = shift(low, up, down), shift(high, back_up, back_down)
    high_before, low_after = shift(high, up, down), shift(low, back_up, back_down)
    product = first_product((low, high), prepared)
    low_before, high_after, *product = together(low_before, high_after, *product)
    low_far, high_far = shift(low_before, up, down), shift(high_after, back_up, back_down)
    return prepared, product, (low_before, high_after), (high_before, low_after), (low_far, high_far)


LOW, HIGH = NEAR[:2], NEAR[2:]
STAGES = (
    [[(a, 0) for a in LOW], [(a, 0) for a in HIGH]],
    [[(a, -1) for a in LOW], [(a, 1) for a in HIGH]],
    [[(a, -1) for a in HIGH], [(a, 1) for a in LOW]],
    [[(a, -2) for a in LOW], [(a, 2) for a in HIGH]],
)
ORDER = [block for stage in STAGES for piece in stage for block in piece]
STAGE_ROWS = [sum(len(piece) for piece in stage) * BLOCK for stage in STAGES]
SENDS = (1, 1, 2, 2)


def wrap(step):
    return -2 if step == 2 else step


def slot(block):
    at = ORDER.index(block) * BLOCK
    for stage, rows in enumerate(STAGE_ROWS):
        if at < rows:
            return stage, at
        at -= rows


def twin(block):
    other = (wrap(block[1]), wrap(block[0]))
    return next(b for b in ORDER if (wrap(b[0]), wrap(b[1])) == other)


def stage_of(block):
    return max(slot(block)[0], slot(twin(block))[0])


EARLY = sorted((block for block in ORDER if stage_of(block) < 3), key=lambda block: stage_of(block) > 1)
LATE = [block for block in ORDER if stage_of(block) == 3]
FIRST = 3


def place_here():
    row = lax.axis_index("rows")
    return row // (NY * NX), (row // NX) & (NY - 1), row & (NX - 1), lax.axis_index("feat")


def depth(core, block):
    return block[1] if block[0] == block[1] else jnp.where(core == 0, block[1], block[0])


def first_rows(place, block):
    z, y, x, core = place[0], place[1], place[2], place[3] & 1
    dz = depth(core, block)
    dy = depth(1 - core, block)
    row = ((z + dz) & (NZ - 1)) * (NY * NX) + ((y + dy) & (NY - 1)) * NX + x
    return [pl.multiple_of((row ^ (NZ // 2 * NY * NX * (part % 2) + part // 2)) * SHARD, SHARD) for part in range(4)]


def twin_rows(place, block):
    core = place[3] & 1
    stage, start = slot(twin(block))
    each = STAGE_ROWS[stage] // SENDS[stage]
    parts = [start % each + part * SHARD for part in range(4)]
    if 2 in (block[1], twin(block)[1]):
        away = (((depth(core, block) - depth(1 - core, twin(block))) >> 2) & 1) * SHARD
        parts = [pl.multiple_of(row ^ away, SHARD) for row in parts]
    return sum(SENDS[:stage]) + start // each, parts


def split3(value):
    high = value.astype(jnp.bfloat16)
    rest = value - high.astype(jnp.float32)
    middle = rest.astype(jnp.bfloat16)
    low = (rest - middle.astype(jnp.float32)).astype(jnp.bfloat16)
    return [high, middle, low]


def copy_kernel(from_ref, to_ref):
    to_ref[...] = from_ref[...]


def prepare_kernel(train_ref, turned_ref, sums_ref):
    me = lax.axis_index("feat")
    for k, mask in enumerate((0, 2, 1, 3)):
        start = pl.multiple_of((me ^ mask) * 256, 256)
        for j in range(0, 2048, 512):
            block = train_ref[pl.ds(start, 256), j : j + 512].T
            turned_ref[k, j : j + 512, :] = block
            wide = block.astype(jnp.float32)
            part = jnp.sum(wide * wide, axis=0, keepdims=True)
            if j == 0:
                sums_ref[k : k + 1, :] = part
            else:
                sums_ref[k : k + 1, :] += part


def condition(pieces, precond_ref, sums_ref, rounded_ref):
    base = 0
    for piece in pieces:
        rows = piece.shape[0]
        here = slice(base, base + rows)
        squares = jnp.zeros((rows, 128), jnp.float32)
        for k in range(8):
            columns = slice(k * 256, (k + 1) * 256)
            value = jnp.dot(piece[:, columns], precond_ref[k], preferred_element_type=jnp.float32)
            rounded_ref[here, columns] = value.astype(jnp.bfloat16)
            value = value * value
            squares += value[:, :128] + value[:, 128:]
        sums_ref[here, :] = squares
        base += rows


def multiply(rounded_ref, turned_ref, refs, first):
    each = rounded_ref.shape[0] // len(refs)
    for k in range(2):
        value = jnp.dot(rounded_ref[...], turned_ref[first + k], preferred_element_type=jnp.float32)
        for n, ref in enumerate(refs):
            ref[:each, k * 256 : (k + 1) * 256] = value[n * each : (n + 1) * each].astype(ref.dtype)


def products_kernel(turned_ref, precond_ref, low, high, keep_ref, *refs):
    *send_refs, sums_ref, rounded_ref = refs
    condition((low, high), precond_ref, sums_ref, rounded_ref)
    multiply(rounded_ref, turned_ref, send_refs, 2)
    multiply(rounded_ref, turned_ref, [keep_ref], 0)


def sent_kernel(turned_ref, precond_ref, low, high, rounded_ref, send_low, send_high, sums_ref):
    condition((low, high), precond_ref, sums_ref, rounded_ref)
    multiply(rounded_ref, turned_ref, [send_low, send_high], 2)


def kept_kernel(turned_ref, rounded_ref, keep_ref):
    multiply(rounded_ref, turned_ref, [keep_ref], 0)


def last_sent_kernel(
    turned_ref, precond_ref, low, high, sums0, sums1, sums2, train_ref, rounded_ref, send_low, send_high, lanes_ref, sums3, all_sums
):
    condition((low, high), precond_ref, sums3, rounded_ref)
    multiply(rounded_ref, turned_ref, [send_low, send_high], 2)
    sums = (sums0, sums1, sums2, sums3)
    place = place_here()
    for block in ORDER:
        stage, at = slot(block)
        for part, row in enumerate(first_rows(place, block)):
            here = slice(at + part * SHARD, at + (part + 1) * SHARD)
            all_sums[pl.ds(row, SHARD), :] = sums[stage][here, :]
    lanes = jnp.sum(all_sums[...].T, axis=0, keepdims=True)
    lanes_ref[...] = lanes
    extra = split3(lanes[:, :512]) + split3(lanes[:, 512:])
    extra += split3(jnp.concatenate([train_ref[2:3, :], train_ref[3:4, :]], axis=1))
    extra.append(jnp.zeros((SHARD - len(extra), 512), jnp.bfloat16))
    send_high[low.shape[0] :, :] = jnp.concatenate(extra, axis=0)


def add_blocks(blocks, keeps, gots, mine_ref, send_ref, at=0):
    first = at
    place = place_here()
    for block in blocks:
        stage, base = slot(block)
        there, rows = twin_rows(place, block)
        for part, row in enumerate(rows):
            own = keeps[stage][base + part * SHARD : base + (part + 1) * SHARD, :]
            total = own + gots[there][pl.ds(row, SHARD), :].astype(jnp.float32)
            mine_ref[at : at + SHARD, :] = total[:, :256]
            send_ref[at - first : at - first + SHARD, :] = total[:, 256:].astype(jnp.bfloat16)
            at += SHARD


def first_kernel(keep0, keep1, got0, got1, mine_ref, send_ref):
    add_blocks(EARLY[:FIRST], (keep0, keep1), (got0, got1), mine_ref, send_ref)


def early_kernel(*refs):
    keeps, gots = refs[: len(STAGES) - 1], refs[len(STAGES) - 1 : -2]
    add_blocks(EARLY[FIRST:], keeps, gots, *refs[-2:])


def late_kernel(*refs):
    first, last = len(STAGES), len(STAGES) + sum(SENDS)
    keeps, gots, rest = refs[:first], refs[first:last], refs[last:]
    lanes_ref, train_ref, mine_ref, send_low, send_high, lanes2_ref, train2_ref = rest
    add_blocks(LATE[:4], keeps, gots, mine_ref, send_low)
    add_blocks(LATE[4:], keeps, gots, mine_ref, send_high, 4 * BLOCK)
    got = gots[-1][keeps[-1].shape[0] // 2 :, :].astype(jnp.float32)
    extra = []
    for j in range(2):
        columns = slice(j * 512, (j + 1) * 512)
        total = lanes_ref[:, columns] + sum3(got, 3 * j)
        lanes2_ref[:, columns] = total
        extra += split3(total[:, :256]) + split3(total[:, 256:])
    train = sum3(got, 6)
    train2_ref[...] = train_ref[0:1, :] + train[:, :256]
    extra += split3(train_ref[1:2, :] + train[:, 256:])
    extra.append(jnp.zeros((SHARD - len(extra), 256), jnp.bfloat16))
    send_high[len(LATE[4:]) * BLOCK :, :] = jnp.concatenate(extra, axis=0)


def sum3(rows, at):
    return rows[at : at + 1] + (rows[at + 1 : at + 2] + rows[at + 2 : at + 3])


def merge_kernel(mine0, mine1, got0, got1, all_ref):
    rows = FIRST * BLOCK
    all_ref[:rows, :] = mine0[...] + got0[...].astype(jnp.float32)
    all_ref[rows:, :] = mine1[...] + got1[...].astype(jnp.float32)


def finish_kernel(early_ref, mine1, got1, got2, lanes_ref, train_ref, out_ref, scale_ref, sums_ref, sem):
    split = got1.shape[0]
    late = mine1.shape[0]
    got = got2[late - split :, :].astype(jnp.float32)
    query = lanes_ref[...] + jnp.concatenate([sum3(got, 3 * j) for j in range(4)], axis=1)
    query = 1.0 / jnp.sqrt(query + EPS)
    for i in range(0, 1024, 128):
        scale_ref[i : i + 128, :] = jnp.broadcast_to(query[:, i : i + 128], (128, 128)).T
    train = (1.0 / jnp.sqrt(train_ref[...] + sum3(got, 12) + EPS)) * math.sqrt(F)
    at = 0
    place = place_here()
    for block in EARLY + LATE:
        for row in first_rows(place, block):
            base = at - len(EARLY) * BLOCK
            if base < 0:
                total = early_ref[at : at + SHARD, :]
            else:
                other = got1[base : base + SHARD, :] if base < split else got2[base - split : base - split + SHARD, :]
                total = mine1[base : base + SHARD, :] + other.astype(jnp.float32)
            rows = pl.ds(row, SHARD)
            scale = scale_ref[rows, :]
            for j in range(0, 256, 128):
                sums_ref[at : at + SHARD, j : j + 128] = total[:, j : j + 128] * scale * train[:, j : j + 128]
            pltpu.make_async_copy(sums_ref.at[at : at + SHARD, :], out_ref.at[rows, :], sem).start()
            at += SHARD
    pltpu.make_async_copy(sums_ref, out_ref, sem).wait()


def call(kernel, outs, inputs, scratch=(), out_spec=VMEM):
    return pl.pallas_call(
        kernel,
        out_shape=[jax.ShapeDtypeStruct(s, d) for s, d in outs],
        in_specs=[VMEM] * len(inputs),
        out_specs=[out_spec] * len(outs),
        scratch_shapes=list(scratch),
        compiler_params=pltpu.CompilerParams(vmem_limit_bytes=24 * MIB),
        cost_estimate=pl.CostEstimate(flops=1, bytes_accessed=1, transcendentals=0),
    )(*inputs)


def on_device(query_grads, train_grads, precond):
    f32, bf16 = jnp.float32, jnp.bfloat16

    def prepare(four):
        train, _ = together(train_grads, four)
        return call(
            prepare_kernel,
            [((4, 2048, 256), bf16), ((4, 256), f32)],
            [train],
            )

    def product(pieces, prepared, sends=1):
        rows = sum(piece.shape[0] for piece in pieces)
        return call(
            products_kernel,
            [((rows, 512), f32), *[((rows // sends, 512), bf16)] * sends, ((rows, 128), f32)],
            [prepared[0], precond, *pieces],
            scratch=[pltpu.VMEM((rows, 2048), bf16)],
        )

    prepared, done, *stages, last = gather(query_grads, prepare, product)
    turned, train_sums = prepared
    keep, send, squares = done
    keeps, gots, sums = [keep], [across(send, 1)], [squares]
    *pieces, _ = together(*stages[0], squares)
    keep, send, squares = product(pieces, prepared)
    keeps.append(keep)
    gots.append(across(send, 1))
    sums.append(squares)
    rows = STAGE_ROWS[2]
    *pieces, _, _ = together(*stages[1], squares, gots[0])
    rounded, send_low, send_high, squares = call(
        sent_kernel,
        [((rows, 2048), bf16), *[((rows // 2, 512), bf16)] * 2, ((rows, 128), f32)],
        [turned, precond, *pieces],
    )
    sums.append(squares)
    first = FIRST * BLOCK
    early = len(EARLY) * BLOCK
    late = len(LATE) * BLOCK
    mine_first, send = call(first_kernel, [((first, 256), f32), ((first, 256), bf16)], [*keeps, *gots])
    got_first = across(send, 2)
    rounded, _ = together(rounded, send)
    keeps.append(call(kept_kernel, [((rows, 512), f32)], [turned, rounded])[0])
    gots += [across(send_low, 1), across(send_high, 1)]
    mine0, send = call(
        early_kernel, [((early - first, 256), f32), ((early - first, 256), bf16)], [*keeps, *gots]
    )
    got0 = across(send, 2)
    low, high, _ = together(*last, send)
    rows = STAGE_ROWS[-1]
    rounded, send_low, send_high, lanes = call(
        last_sent_kernel,
        [((rows, 2048), bf16), ((rows // 2, 512), bf16), ((rows // 2 + SHARD, 512), bf16), ((1, 1024), f32)],
        [turned, precond, low, high, *sums, train_sums],
        scratch=[pltpu.VMEM((rows, 128), f32), pltpu.VMEM((1024, 128), f32)],
    )
    keeps.append(call(kept_kernel, [((rows, 512), f32)], [turned, rounded])[0])
    send_low, send_high, got_first = together(send_low, send_high, got_first)
    gots += [across(send_low, 1), across(send_high, 1)]
    mine1, send_low, send_high, lanes, train = call(
        late_kernel,
        [
            ((late, 256), f32),
            ((4 * BLOCK, 256), bf16),
            ((late - 4 * BLOCK + SHARD, 256), bf16),
            ((1, 1024), f32),
            ((1, 256), f32),
        ],
        [*keeps, *gots, lanes, train_sums],
    )
    send_high, got0 = together(send_high, got0)
    got1, got2 = across(send_low, 2), across(send_high, 2)
    merged = call(merge_kernel, [((early, 256), f32)], [mine_first, mine0, got_first, got0])[0]
    return call(
        finish_kernel,
        [((1024, 256), f32)],
        [merged, mine1, got1, got2, lanes, train],
        scratch=[pltpu.VMEM((1024, 128), f32), pltpu.VMEM((1024, 256), f32), pltpu.SemaphoreType.DMA],
        out_spec=pl.BlockSpec(memory_space=pl.ANY),
    )[0]


def solution(mesh):
    in_specs = (P("rows", "feat"), P("rows", "feat"), P("feat", None, None))
    out_specs = P(None, ("rows", "feat"))
    return jax.shard_map(
        on_device, mesh=mesh, in_specs=in_specs, out_specs=out_specs, check_vma=False
    )
```

```python
import math

import jax
import jax.numpy as jnp
from jax import lax
from jax.experimental import pallas as pl
from jax.experimental.pallas import tpu as pltpu
from jax.sharding import PartitionSpec as P

F = 8192
EPS = 1e-06
NZ, NY, NX = 8, 4, 2
SHARD = 16
BLOCK = 4 * SHARD
NEAR = (0, -1, 1, -2)
VMEM = pl.BlockSpec(memory_space=pltpu.VMEM)
MIB = 1 << 20


def row_index(z, y, x):
    return (z % NZ) * (NY * NX) + (y % NY) * NX + x % NX


def shift(value, even, odd=None):
    odd = even if odd is None else odd
    pairs = []
    for z in range(NZ):
        for y in range(NY):
            for x in range(NX):
                for f in range(4):
                    dz, dy, dx = odd if f % 2 else even
                    there = row_index(z + dz, y + dy, x + dx)
                    pairs.append((row_index(z, y, x) * 4 + f, there * 4 + f))
    return lax.ppermute(value, ("rows", "feat"), pairs)


def across(value, mask):
    return lax.ppermute(value, "feat", [(f, f ^ mask) for f in range(4)])


def join(*parts):
    return jnp.concatenate(parts, axis=0)


def together(*values):
    return lax.optimization_barrier(values)


def gather(own, early, first_product):
    near = call(copy_kernel, [(own.shape, own.dtype)], [own])[0]
    pair = join(near, shift(own, (4, 0, 0)))
    four = join(pair, shift(pair, (0, 0, 1)))
    first = [
        shift(four, (0, 1, 0), (1, 0, 0)),
        shift(four, (0, -1, 0), (-1, 0, 0)),
        shift(four, (0, 2, 0), (2, 0, 0)),
    ]
    prepared = early(four)
    low, high, *prepared = together(join(four, first[0]), join(*first[1:]), *prepared)
    up, down = (1, 0, 0), (0, 1, 0)
    back_up, back_down = (-1, 0, 0), (0, -1, 0)
    low_before, high_after = shift(low, up, down), shift(high, back_up, back_down)
    high_before, low_after = shift(high, up, down), shift(low, back_up, back_down)
    product = first_product((low, high), prepared)
    low_before, high_after, *product = together(low_before, high_after, *product)
    low_far, high_far = shift(low_before, up, down), shift(high_after, back_up, back_down)
    return prepared, product, (low_before, high_after), (high_before, low_after), (low_far, high_far)


LOW, HIGH = NEAR[:2], NEAR[2:]
STAGES = (
    [[(a, 0) for a in LOW], [(a, 0) for a in HIGH]],
    [[(a, -1) for a in LOW], [(a, 1) for a in HIGH]],
    [[(a, -1) for a in HIGH], [(a, 1) for a in LOW]],
    [[(a, -2) for a in LOW], [(a, 2) for a in HIGH]],
)
ORDER = [block for stage in STAGES for piece in stage for block in piece]
STAGE_ROWS = [sum(len(piece) for piece in stage) * BLOCK for stage in STAGES]
SENDS = (1, 1, 2, 2)


def wrap(step):
    return -2 if step == 2 else step


def slot(block):
    at = ORDER.index(block) * BLOCK
    for stage, rows in enumerate(STAGE_ROWS):
        if at < rows:
            return stage, at
        at -= rows


def twin(block):
    other = (wrap(block[1]), wrap(block[0]))
    return next(b for b in ORDER if (wrap(b[0]), wrap(b[1])) == other)


def stage_of(block):
    return max(slot(block)[0], slot(twin(block))[0])


EARLY = sorted((block for block in ORDER if stage_of(block) < 3), key=lambda block: stage_of(block) > 1)
LATE = [block for block in ORDER if stage_of(block) == 3]


def place_here():
    row = lax.axis_index("rows")
    return row // (NY * NX), (row // NX) & (NY - 1), row & (NX - 1), lax.axis_index("feat")


def depth(core, block):
    return block[1] if block[0] == block[1] else jnp.where(core == 0, block[1], block[0])


def first_rows(place, block):
    z, y, x, core = place[0], place[1], place[2], place[3] & 1
    dz = depth(core, block)
    dy = depth(1 - core, block)
    row = ((z + dz) & (NZ - 1)) * (NY * NX) + ((y + dy) & (NY - 1)) * NX + x
    return [pl.multiple_of((row ^ (NZ // 2 * NY * NX * (part % 2) + part // 2)) * SHARD, SHARD) for part in range(4)]


def twin_rows(place, block):
    core = place[3] & 1
    stage, start = slot(twin(block))
    each = STAGE_ROWS[stage] // SENDS[stage]
    parts = [start % each + part * SHARD for part in range(4)]
    if 2 in (block[1], twin(block)[1]):
        away = (((depth(core, block) - depth(1 - core, twin(block))) >> 2) & 1) * SHARD
        parts = [pl.multiple_of(row ^ away, SHARD) for row in parts]
    return sum(SENDS[:stage]) + start // each, parts


def split3(value):
    high = value.astype(jnp.bfloat16)
    rest = value - high.astype(jnp.float32)
    middle = rest.astype(jnp.bfloat16)
    low = (rest - middle.astype(jnp.float32)).astype(jnp.bfloat16)
    return [high, middle, low]


def copy_kernel(from_ref, to_ref):
    to_ref[...] = from_ref[...]


def prepare_kernel(train_ref, turned_ref, sums_ref):
    me = lax.axis_index("feat")
    for k, mask in enumerate((0, 2, 1, 3)):
        start = pl.multiple_of((me ^ mask) * 256, 256)
        for j in range(0, 2048, 512):
            block = train_ref[pl.ds(start, 256), j : j + 512].T
            turned_ref[k, j : j + 512, :] = block
            wide = block.astype(jnp.float32)
            part = jnp.sum(wide * wide, axis=0, keepdims=True)
            if j == 0:
                sums_ref[k : k + 1, :] = part
            else:
                sums_ref[k : k + 1, :] += part


def condition(pieces, precond_ref, sums_ref, rounded_ref):
    base = 0
    for piece in pieces:
        rows = piece.shape[0]
        here = slice(base, base + rows)
        squares = jnp.zeros((rows, 128), jnp.float32)
        for k in range(8):
            columns = slice(k * 256, (k + 1) * 256)
            value = jnp.dot(piece[:, columns], precond_ref[k], preferred_element_type=jnp.float32)
            rounded_ref[here, columns] = value.astype(jnp.bfloat16)
            value = value * value
            squares += value[:, :128] + value[:, 128:]
        sums_ref[here, :] = squares
        base += rows


def multiply(rounded_ref, turned_ref, refs, first):
    each = rounded_ref.shape[0] // len(refs)
    for k in range(2):
        value = jnp.dot(rounded_ref[...], turned_ref[first + k], preferred_element_type=jnp.float32)
        for n, ref in enumerate(refs):
            ref[:each, k * 256 : (k + 1) * 256] = value[n * each : (n + 1) * each].astype(ref.dtype)


def products_kernel(turned_ref, precond_ref, low, high, keep_ref, *refs):
    *send_refs, sums_ref, rounded_ref = refs
    condition((low, high), precond_ref, sums_ref, rounded_ref)
    multiply(rounded_ref, turned_ref, send_refs, 2)
    multiply(rounded_ref, turned_ref, [keep_ref], 0)


def sent_kernel(turned_ref, precond_ref, low, high, rounded_ref, send_low, send_high, sums_ref):
    condition((low, high), precond_ref, sums_ref, rounded_ref)
    multiply(rounded_ref, turned_ref, [send_low, send_high], 2)


def kept_kernel(turned_ref, rounded_ref, keep_ref):
    multiply(rounded_ref, turned_ref, [keep_ref], 0)


def last_sent_kernel(
    turned_ref, precond_ref, low, high, sums0, sums1, sums2, train_ref, rounded_ref, send_low, send_high, lanes_ref, sums3, all_sums
):
    condition((low, high), precond_ref, sums3, rounded_ref)
    multiply(rounded_ref, turned_ref, [send_low, send_high], 2)
    sums = (sums0, sums1, sums2, sums3)
    place = place_here()
    for block in ORDER:
        stage, at = slot(block)
        for part, row in enumerate(first_rows(place, block)):
            here = slice(at + part * SHARD, at + (part + 1) * SHARD)
            all_sums[pl.ds(row, SHARD), :] = sums[stage][here, :]
    lanes = jnp.sum(all_sums[...].T, axis=0, keepdims=True)
    lanes_ref[...] = lanes
    extra = split3(lanes[:, :512]) + split3(lanes[:, 512:])
    extra += split3(jnp.concatenate([train_ref[2:3, :], train_ref[3:4, :]], axis=1))
    extra.append(jnp.zeros((SHARD - len(extra), 512), jnp.bfloat16))
    send_high[low.shape[0] :, :] = jnp.concatenate(extra, axis=0)


def add_blocks(blocks, keeps, gots, mine_ref, send_ref, at=0):
    first = at
    place = place_here()
    for block in blocks:
        stage, base = slot(block)
        there, rows = twin_rows(place, block)
        for part, row in enumerate(rows):
            own = keeps[stage][base + part * SHARD : base + (part + 1) * SHARD, :]
            total = own + gots[there][pl.ds(row, SHARD), :].astype(jnp.float32)
            mine_ref[at : at + SHARD, :] = total[:, :256]
            send_ref[at - first : at - first + SHARD, :] = total[:, 256:].astype(jnp.bfloat16)
            at += SHARD


def early_kernel(*refs):
    keeps, gots = refs[: len(STAGES) - 1], refs[len(STAGES) - 1 : -2]
    add_blocks(EARLY, keeps, gots, *refs[-2:])


def late_kernel(*refs):
    first, last = len(STAGES), len(STAGES) + sum(SENDS)
    keeps, gots, rest = refs[:first], refs[first:last], refs[last:]
    lanes_ref, train_ref, mine_ref, send_low, send_high, lanes2_ref, train2_ref = rest
    add_blocks(LATE[:4], keeps, gots, mine_ref, send_low)
    add_blocks(LATE[4:], keeps, gots, mine_ref, send_high, 4 * BLOCK)
    got = gots[-1][keeps[-1].shape[0] // 2 :, :].astype(jnp.float32)
    extra = []
    for j in range(2):
        columns = slice(j * 512, (j + 1) * 512)
        total = lanes_ref[:, columns] + sum3(got, 3 * j)
        lanes2_ref[:, columns] = total
        extra += split3(total[:, :256]) + split3(total[:, 256:])
    train = sum3(got, 6)
    train2_ref[...] = train_ref[0:1, :] + train[:, :256]
    extra += split3(train_ref[1:2, :] + train[:, 256:])
    extra.append(jnp.zeros((SHARD - len(extra), 256), jnp.bfloat16))
    send_high[len(LATE[4:]) * BLOCK :, :] = jnp.concatenate(extra, axis=0)


def sum3(rows, at):
    return rows[at : at + 1] + (rows[at + 1 : at + 2] + rows[at + 2 : at + 3])


def merge_kernel(mine0, got0, all_ref):
    all_ref[...] = mine0[...] + got0[...].astype(jnp.float32)


def finish_kernel(early_ref, mine1, got1, got2, lanes_ref, train_ref, out_ref, scale_ref, sums_ref, sem):
    split = got1.shape[0]
    late = mine1.shape[0]
    got = got2[late - split :, :].astype(jnp.float32)
    query = lanes_ref[...] + jnp.concatenate([sum3(got, 3 * j) for j in range(4)], axis=1)
    query = 1.0 / jnp.sqrt(query + EPS)
    for i in range(0, 1024, 128):
        scale_ref[i : i + 128, :] = jnp.broadcast_to(query[:, i : i + 128], (128, 128)).T
    train = (1.0 / jnp.sqrt(train_ref[...] + sum3(got, 12) + EPS)) * math.sqrt(F)
    at = 0
    place = place_here()
    for block in EARLY + LATE:
        for row in first_rows(place, block):
            base = at - len(EARLY) * BLOCK
            if base < 0:
                total = early_ref[at : at + SHARD, :]
            else:
                other = got1[base : base + SHARD, :] if base < split else got2[base - split : base - split + SHARD, :]
                total = mine1[base : base + SHARD, :] + other.astype(jnp.float32)
            rows = pl.ds(row, SHARD)
            scale = scale_ref[rows, :]
            for j in range(0, 256, 128):
                sums_ref[at : at + SHARD, j : j + 128] = total[:, j : j + 128] * scale * train[:, j : j + 128]
            pltpu.make_async_copy(sums_ref.at[at : at + SHARD, :], out_ref.at[rows, :], sem).start()
            at += SHARD
    pltpu.make_async_copy(sums_ref, out_ref, sem).wait()


def call(kernel, outs, inputs, scratch=(), out_spec=VMEM):
    return pl.pallas_call(
        kernel,
        out_shape=[jax.ShapeDtypeStruct(s, d) for s, d in outs],
        in_specs=[VMEM] * len(inputs),
        out_specs=[out_spec] * len(outs),
        scratch_shapes=list(scratch),
        compiler_params=pltpu.CompilerParams(vmem_limit_bytes=24 * MIB),
        cost_estimate=pl.CostEstimate(flops=1, bytes_accessed=1, transcendentals=0),
    )(*inputs)


def on_device(query_grads, train_grads, precond):
    f32, bf16 = jnp.float32, jnp.bfloat16

    def prepare(four):
        train, _ = together(train_grads, four)
        return call(
            prepare_kernel,
            [((4, 2048, 256), bf16), ((4, 256), f32)],
            [train],
            )

    def product(pieces, prepared, sends=1):
        rows = sum(piece.shape[0] for piece in pieces)
        return call(
            products_kernel,
            [((rows, 512), f32), *[((rows // sends, 512), bf16)] * sends, ((rows, 128), f32)],
            [prepared[0], precond, *pieces],
            scratch=[pltpu.VMEM((rows, 2048), bf16)],
        )

    prepared, done, *stages, last = gather(query_grads, prepare, product)
    turned, train_sums = prepared
    keep, send, squares = done
    keeps, gots, sums = [keep], [across(send, 1)], [squares]
    *pieces, _ = together(*stages[0], squares)
    keep, send, squares = product(pieces, prepared)
    keeps.append(keep)
    gots.append(across(send, 1))
    sums.append(squares)
    rows = STAGE_ROWS[2]
    *pieces, _, _ = together(*stages[1], squares, gots[0])
    rounded, send_low, send_high, squares = call(
        sent_kernel,
        [((rows, 2048), bf16), *[((rows // 2, 512), bf16)] * 2, ((rows, 128), f32)],
        [turned, precond, *pieces],
    )
    sums.append(squares)
    early = len(EARLY) * BLOCK
    late = len(LATE) * BLOCK
    keeps.append(call(kept_kernel, [((rows, 512), f32)], [turned, rounded])[0])
    gots += [across(send_low, 1), across(send_high, 1)]
    mine0, send = call(early_kernel, [((early, 256), f32), ((early, 256), bf16)], [*keeps, *gots])
    got0 = across(send, 2)
    low, high, _ = together(*last, send)
    rows = STAGE_ROWS[-1]
    rounded, send_low, send_high, lanes = call(
        last_sent_kernel,
        [((rows, 2048), bf16), ((rows // 2, 512), bf16), ((rows // 2 + SHARD, 512), bf16), ((1, 1024), f32)],
        [turned, precond, low, high, *sums, train_sums],
        scratch=[pltpu.VMEM((rows, 128), f32), pltpu.VMEM((1024, 128), f32)],
    )
    keeps.append(call(kept_kernel, [((rows, 512), f32)], [turned, rounded])[0])
    gots += [across(send_low, 1), across(send_high, 1)]
    mine1, send_low, send_high, lanes, train = call(
        late_kernel,
        [
            ((late, 256), f32),
            ((4 * BLOCK, 256), bf16),
            ((late - 4 * BLOCK + SHARD, 256), bf16),
            ((1, 1024), f32),
            ((1, 256), f32),
        ],
        [*keeps, *gots, lanes, train_sums],
    )
    got1, got2 = across(send_low, 2), across(send_high, 2)
    merged = call(merge_kernel, [((early, 256), f32)], [mine0, got0])[0]
    return call(
        finish_kernel,
        [((1024, 256), f32)],
        [merged, mine1, got1, got2, lanes, train],
        scratch=[pltpu.VMEM((1024, 128), f32), pltpu.VMEM((1024, 256), f32), pltpu.SemaphoreType.DMA],
        out_spec=pl.BlockSpec(memory_space=pl.ANY),
    )[0]


def solution(mesh):
    in_specs = (P("rows", "feat"), P("rows", "feat"), P("feat", None, None))
    out_specs = P(None, ("rows", "feat"))
    return jax.shard_map(
        on_device, mesh=mesh, in_specs=in_specs, out_specs=out_specs, check_vma=False
    )
```

```python
import math

import jax
import jax.numpy as jnp
from jax import lax
from jax.experimental import pallas as pl
from jax.experimental.pallas import tpu as pltpu
from jax.sharding import PartitionSpec as P

F = 8192
EPS = 1e-06
NZ, NY, NX = 8, 4, 2
SHARD = 16
BLOCK = 4 * SHARD
NEAR = (0, -1, 1, -2)
VMEM = pl.BlockSpec(memory_space=pltpu.VMEM)
MIB = 1 << 20


def row_index(z, y, x):
    return (z % NZ) * (NY * NX) + (y % NY) * NX + x % NX


def shift(value, even, odd=None):
    odd = even if odd is None else odd
    pairs = []
    for z in range(NZ):
        for y in range(NY):
            for x in range(NX):
                for f in range(4):
                    dz, dy, dx = odd if f % 2 else even
                    there = row_index(z + dz, y + dy, x + dx)
                    pairs.append((row_index(z, y, x) * 4 + f, there * 4 + f))
    return lax.ppermute(value, ("rows", "feat"), pairs)


def across(value, mask):
    return lax.ppermute(value, "feat", [(f, f ^ mask) for f in range(4)])


def join(*parts):
    return jnp.concatenate(parts, axis=0)


def together(*values):
    return lax.optimization_barrier(values)


def gather(own, early, first_product):
    near = call(copy_kernel, [(own.shape, own.dtype)], [own])[0]
    pair = join(near, shift(own, (4, 0, 0)))
    four = join(pair, shift(pair, (0, 0, 1)))
    first = [
        shift(four, (0, 1, 0), (1, 0, 0)),
        shift(four, (0, -1, 0), (-1, 0, 0)),
        shift(four, (0, 2, 0), (2, 0, 0)),
    ]
    prepared = early(four)
    low, high, *prepared = together(join(four, first[0]), join(*first[1:]), *prepared)
    up, down = (1, 0, 0), (0, 1, 0)
    back_up, back_down = (-1, 0, 0), (0, -1, 0)
    low_before, high_after = shift(low, up, down), shift(high, back_up, back_down)
    high_before, low_after = shift(high, up, down), shift(low, back_up, back_down)
    product = first_product((low, high), prepared)
    low_before, high_after, *product = together(low_before, high_after, *product)
    low_far, high_far = shift(low_before, up, down), shift(high_after, back_up, back_down)
    return prepared, product, (low_before, high_after), (high_before, low_after), (low_far, high_far)


LOW, HIGH = NEAR[:2], NEAR[2:]
STAGES = (
    [[(a, 0) for a in LOW], [(a, 0) for a in HIGH]],
    [[(a, -1) for a in LOW], [(a, 1) for a in HIGH]],
    [[(a, -1) for a in HIGH], [(a, 1) for a in LOW]],
    [[(a, -2) for a in LOW], [(a, 2) for a in HIGH]],
)
ORDER = [block for stage in STAGES for piece in stage for block in piece]
STAGE_ROWS = [sum(len(piece) for piece in stage) * BLOCK for stage in STAGES]
SENDS = (1, 1, 2, 2)


def wrap(step):
    return -2 if step == 2 else step


def slot(block):
    at = ORDER.index(block) * BLOCK
    for stage, rows in enumerate(STAGE_ROWS):
        if at < rows:
            return stage, at
        at -= rows


def twin(block):
    other = (wrap(block[1]), wrap(block[0]))
    return next(b for b in ORDER if (wrap(b[0]), wrap(b[1])) == other)


def stage_of(block):
    return max(slot(block)[0], slot(twin(block))[0])


EARLY = sorted((block for block in ORDER if stage_of(block) < 3), key=lambda block: stage_of(block) > 1)
LATE = [block for block in ORDER if stage_of(block) == 3]


def place_here():
    row = lax.axis_index("rows")
    return row // (NY * NX), (row // NX) & (NY - 1), row & (NX - 1), lax.axis_index("feat")


def depth(core, block):
    return block[1] if block[0] == block[1] else jnp.where(core == 0, block[1], block[0])


def first_rows(place, block):
    z, y, x, core = place[0], place[1], place[2], place[3] & 1
    dz = depth(core, block)
    dy = depth(1 - core, block)
    row = ((z + dz) & (NZ - 1)) * (NY * NX) + ((y + dy) & (NY - 1)) * NX + x
    return [pl.multiple_of((row ^ (NZ // 2 * NY * NX * (part % 2) + part // 2)) * SHARD, SHARD) for part in range(4)]


def twin_rows(place, block):
    core = place[3] & 1
    stage, start = slot(twin(block))
    each = STAGE_ROWS[stage] // SENDS[stage]
    parts = [start % each + part * SHARD for part in range(4)]
    if 2 in (block[1], twin(block)[1]):
        away = (((depth(core, block) - depth(1 - core, twin(block))) >> 2) & 1) * SHARD
        parts = [pl.multiple_of(row ^ away, SHARD) for row in parts]
    return sum(SENDS[:stage]) + start // each, parts


def split3(value):
    high = value.astype(jnp.bfloat16)
    rest = value - high.astype(jnp.float32)
    middle = rest.astype(jnp.bfloat16)
    low = (rest - middle.astype(jnp.float32)).astype(jnp.bfloat16)
    return [high, middle, low]


def copy_kernel(from_ref, to_ref):
    to_ref[...] = from_ref[...]


def prepare_kernel(train_ref, turned_ref, sums_ref):
    me = lax.axis_index("feat")
    for k, mask in enumerate((0, 2, 1, 3)):
        start = pl.multiple_of((me ^ mask) * 256, 256)
        for j in range(0, 2048, 512):
            block = train_ref[pl.ds(start, 256), j : j + 512].T
            turned_ref[k, j : j + 512, :] = block
            wide = block.astype(jnp.float32)
            part = jnp.sum(wide * wide, axis=0, keepdims=True)
            if j == 0:
                sums_ref[k : k + 1, :] = part
            else:
                sums_ref[k : k + 1, :] += part


def condition(pieces, precond_ref, sums_ref, rounded_ref):
    base = 0
    for piece in pieces:
        rows = piece.shape[0]
        here = slice(base, base + rows)
        squares = jnp.zeros((rows, 128), jnp.float32)
        for k in range(8):
            columns = slice(k * 256, (k + 1) * 256)
            value = jnp.dot(piece[:, columns], precond_ref[k], preferred_element_type=jnp.float32)
            rounded_ref[here, columns] = value.astype(jnp.bfloat16)
            value = value * value
            squares += value[:, :128] + value[:, 128:]
        sums_ref[here, :] = squares
        base += rows


def multiply(rounded_ref, turned_ref, refs, first):
    each = rounded_ref.shape[0] // len(refs)
    for k in range(2):
        value = jnp.dot(rounded_ref[...], turned_ref[first + k], preferred_element_type=jnp.float32)
        for n, ref in enumerate(refs):
            ref[:each, k * 256 : (k + 1) * 256] = value[n * each : (n + 1) * each].astype(ref.dtype)


def products_kernel(turned_ref, precond_ref, low, high, keep_ref, *refs):
    *send_refs, sums_ref, rounded_ref = refs
    condition((low, high), precond_ref, sums_ref, rounded_ref)
    multiply(rounded_ref, turned_ref, send_refs, 2)
    multiply(rounded_ref, turned_ref, [keep_ref], 0)


def sent_kernel(turned_ref, precond_ref, low, high, rounded_ref, send_low, send_high, sums_ref):
    condition((low, high), precond_ref, sums_ref, rounded_ref)
    multiply(rounded_ref, turned_ref, [send_low, send_high], 2)


def kept_kernel(turned_ref, rounded_ref, keep_ref):
    multiply(rounded_ref, turned_ref, [keep_ref], 0)


def last_sent_kernel(
    turned_ref, precond_ref, low, high, sums0, sums1, sums2, train_ref, rounded_ref, send_low, send_high, lanes_ref, sums3, all_sums
):
    condition((low, high), precond_ref, sums3, rounded_ref)
    multiply(rounded_ref, turned_ref, [send_low, send_high], 2)
    sums = (sums0, sums1, sums2, sums3)
    place = place_here()
    for block in ORDER:
        stage, at = slot(block)
        for part, row in enumerate(first_rows(place, block)):
            here = slice(at + part * SHARD, at + (part + 1) * SHARD)
            all_sums[pl.ds(row, SHARD), :] = sums[stage][here, :]
    lanes = jnp.sum(all_sums[...].T, axis=0, keepdims=True)
    lanes_ref[...] = lanes
    extra = split3(lanes[:, :512]) + split3(lanes[:, 512:])
    extra += split3(jnp.concatenate([train_ref[2:3, :], train_ref[3:4, :]], axis=1))
    extra.append(jnp.zeros((SHARD - len(extra), 512), jnp.bfloat16))
    send_high[low.shape[0] :, :] = jnp.concatenate(extra, axis=0)


def add_blocks(blocks, keeps, gots, mine_ref, send_ref, at=0):
    first = at
    place = place_here()
    for block in blocks:
        stage, base = slot(block)
        there, rows = twin_rows(place, block)
        for part, row in enumerate(rows):
            own = keeps[stage][base + part * SHARD : base + (part + 1) * SHARD, :]
            total = own + gots[there][pl.ds(row, SHARD), :].astype(jnp.float32)
            mine_ref[at : at + SHARD, :] = total[:, :256]
            send_ref[at - first : at - first + SHARD, :] = total[:, 256:].astype(jnp.bfloat16)
            at += SHARD


def early_kernel(*refs):
    keeps, gots = refs[: len(STAGES) - 1], refs[len(STAGES) - 1 : -2]
    add_blocks(EARLY, keeps, gots, *refs[-2:])


def late_kernel(*refs):
    first, last = len(STAGES), len(STAGES) + sum(SENDS)
    keeps, gots, rest = refs[:first], refs[first:last], refs[last:]
    lanes_ref, train_ref, mine_ref, send_low, send_high, lanes2_ref, train2_ref = rest
    add_blocks(LATE[:4], keeps, gots, mine_ref, send_low)
    add_blocks(LATE[4:], keeps, gots, mine_ref, send_high, 4 * BLOCK)
    got = gots[-1][keeps[-1].shape[0] // 2 :, :].astype(jnp.float32)
    extra = []
    for j in range(2):
        columns = slice(j * 512, (j + 1) * 512)
        total = lanes_ref[:, columns] + sum3(got, 3 * j)
        lanes2_ref[:, columns] = total
        extra += split3(total[:, :256]) + split3(total[:, 256:])
    train = sum3(got, 6)
    train2_ref[...] = train_ref[0:1, :] + train[:, :256]
    extra += split3(train_ref[1:2, :] + train[:, 256:])
    extra.append(jnp.zeros((SHARD - len(extra), 256), jnp.bfloat16))
    send_high[len(LATE[4:]) * BLOCK :, :] = jnp.concatenate(extra, axis=0)


def sum3(rows, at):
    return rows[at : at + 1] + (rows[at + 1 : at + 2] + rows[at + 2 : at + 3])


def merge_kernel(mine0, got0, all_ref):
    all_ref[...] = mine0[...] + got0[...].astype(jnp.float32)


def finish_kernel(early_ref, mine1, got1, got2, lanes_ref, train_ref, out_ref, scale_ref, sums_ref, sem):
    split = got1.shape[0]
    late = mine1.shape[0]
    got = got2[late - split :, :].astype(jnp.float32)
    query = lanes_ref[...] + jnp.concatenate([sum3(got, 3 * j) for j in range(4)], axis=1)
    query = 1.0 / jnp.sqrt(query + EPS)
    for i in range(0, 1024, 128):
        scale_ref[i : i + 128, :] = jnp.broadcast_to(query[:, i : i + 128], (128, 128)).T
    train = (1.0 / jnp.sqrt(train_ref[...] + sum3(got, 12) + EPS)) * math.sqrt(F)
    at = 0
    place = place_here()
    for block in EARLY + LATE:
        for row in first_rows(place, block):
            base = at - len(EARLY) * BLOCK
            if base < 0:
                total = early_ref[at : at + SHARD, :]
            else:
                other = got1[base : base + SHARD, :] if base < split else got2[base - split : base - split + SHARD, :]
                total = mine1[base : base + SHARD, :] + other.astype(jnp.float32)
            rows = pl.ds(row, SHARD)
            scale = scale_ref[rows, :]
            for j in range(0, 256, 128):
                sums_ref[at : at + SHARD, j : j + 128] = total[:, j : j + 128] * scale * train[:, j : j + 128]
            pltpu.make_async_copy(sums_ref.at[at : at + SHARD, :], out_ref.at[rows, :], sem).start()
            at += SHARD
    pltpu.make_async_copy(sums_ref, out_ref, sem).wait()


def call(kernel, outs, inputs, scratch=(), out_spec=VMEM):
    return pl.pallas_call(
        kernel,
        out_shape=[jax.ShapeDtypeStruct(s, d) for s, d in outs],
        in_specs=[VMEM] * len(inputs),
        out_specs=[out_spec] * len(outs),
        scratch_shapes=list(scratch),
        compiler_params=pltpu.CompilerParams(vmem_limit_bytes=24 * MIB),
        cost_estimate=pl.CostEstimate(flops=1, bytes_accessed=1, transcendentals=0),
    )(*inputs)


def on_device(query_grads, train_grads, precond):
    f32, bf16 = jnp.float32, jnp.bfloat16

    def prepare(four):
        train, _ = together(train_grads, four)
        return call(
            prepare_kernel,
            [((4, 2048, 256), bf16), ((4, 256), f32)],
            [train],
            )

    def product(pieces, prepared, sends=1):
        rows = sum(piece.shape[0] for piece in pieces)
        return call(
            products_kernel,
            [((rows, 512), f32), *[((rows // sends, 512), bf16)] * sends, ((rows, 128), f32)],
            [prepared[0], precond, *pieces],
            scratch=[pltpu.VMEM((rows, 2048), bf16)],
        )

    prepared, done, *stages, last = gather(query_grads, prepare, product)
    turned, train_sums = prepared
    keep, send, squares = done
    keeps, sums = [keep], [squares]
    *pieces, _ = together(*stages[0], squares)
    keep, send1, squares = product(pieces, prepared)
    keeps.append(keep)
    sums.append(squares)
    send, _ = together(send, squares)
    gots = [across(send, 1), across(send1, 1)]
    rows = STAGE_ROWS[2]
    *pieces, _, _ = together(*stages[1], squares, gots[0])
    rounded, send_low, send_high, squares = call(
        sent_kernel,
        [((rows, 2048), bf16), *[((rows // 2, 512), bf16)] * 2, ((rows, 128), f32)],
        [turned, precond, *pieces],
    )
    sums.append(squares)
    early = len(EARLY) * BLOCK
    late = len(LATE) * BLOCK
    keeps.append(call(kept_kernel, [((rows, 512), f32)], [turned, rounded])[0])
    gots += [across(send_low, 1), across(send_high, 1)]
    mine0, send = call(early_kernel, [((early, 256), f32), ((early, 256), bf16)], [*keeps, *gots])
    got0 = across(send, 2)
    low, high, _ = together(*last, send)
    rows = STAGE_ROWS[-1]
    rounded, send_low, send_high, lanes = call(
        last_sent_kernel,
        [((rows, 2048), bf16), ((rows // 2, 512), bf16), ((rows // 2 + SHARD, 512), bf16), ((1, 1024), f32)],
        [turned, precond, low, high, *sums, train_sums],
        scratch=[pltpu.VMEM((rows, 128), f32), pltpu.VMEM((1024, 128), f32)],
    )
    keeps.append(call(kept_kernel, [((rows, 512), f32)], [turned, rounded])[0])
    gots += [across(send_low, 1), across(send_high, 1)]
    mine1, send_low, send_high, lanes, train = call(
        late_kernel,
        [
            ((late, 256), f32),
            ((4 * BLOCK, 256), bf16),
            ((late - 4 * BLOCK + SHARD, 256), bf16),
            ((1, 1024), f32),
            ((1, 256), f32),
        ],
        [*keeps, *gots, lanes, train_sums],
    )
    got1, got2 = across(send_low, 2), across(send_high, 2)
    merged = call(merge_kernel, [((early, 256), f32)], [mine0, got0])[0]
    return call(
        finish_kernel,
        [((1024, 256), f32)],
        [merged, mine1, got1, got2, lanes, train],
        scratch=[pltpu.VMEM((1024, 128), f32), pltpu.VMEM((1024, 256), f32), pltpu.SemaphoreType.DMA],
        out_spec=pl.BlockSpec(memory_space=pl.ANY),
    )[0]


def solution(mesh):
    in_specs = (P("rows", "feat"), P("rows", "feat"), P("feat", None, None))
    out_specs = P(None, ("rows", "feat"))
    return jax.shard_map(
        on_device, mesh=mesh, in_specs=in_specs, out_specs=out_specs, check_vma=False
    )
```

```python
import math

import jax
import jax.numpy as jnp
from jax import lax
from jax.experimental import pallas as pl
from jax.experimental.pallas import tpu as pltpu
from jax.sharding import PartitionSpec as P

F = 8192
EPS = 1e-06
NZ, NY, NX = 8, 4, 2
SHARD = 16
BLOCK = 4 * SHARD
NEAR = (0, -1, 1, -2)
VMEM = pl.BlockSpec(memory_space=pltpu.VMEM)
MIB = 1 << 20


def row_index(z, y, x):
    return (z % NZ) * (NY * NX) + (y % NY) * NX + x % NX


def shift(value, even, odd=None):
    odd = even if odd is None else odd
    pairs = []
    for z in range(NZ):
        for y in range(NY):
            for x in range(NX):
                for f in range(4):
                    dz, dy, dx = odd if f % 2 else even
                    way = -1 if f % 2 else 1
                    there = row_index(z + way * dz, y + way * dy, x + dx)
                    pairs.append((row_index(z, y, x) * 4 + f, there * 4 + f))
    return lax.ppermute(value, ("rows", "feat"), pairs)


def across(value, mask):
    return lax.ppermute(value, "feat", [(f, f ^ mask) for f in range(4)])


def join(*parts):
    return jnp.concatenate(parts, axis=0)


def together(*values):
    return lax.optimization_barrier(values)


def gather(own, early, first_product):
    near = call(copy_kernel, [(own.shape, own.dtype)], [own])[0]
    pair = join(near, shift(own, (4, 0, 0)))
    four = join(pair, shift(pair, (0, 0, 1)))
    first = [
        shift(four, (0, 1, 0), (1, 0, 0)),
        shift(four, (0, -1, 0), (-1, 0, 0)),
        shift(four, (0, 2, 0), (2, 0, 0)),
    ]
    prepared = early(four)
    low, high, *prepared = together(join(four, first[0]), join(*first[1:]), *prepared)
    up, down = (1, 0, 0), (0, 1, 0)
    back_up, back_down = (-1, 0, 0), (0, -1, 0)
    low_before, high_after = shift(low, up, down), shift(high, back_up, back_down)
    high_before, low_after = shift(high, up, down), shift(low, back_up, back_down)
    product = first_product((low, high), prepared)
    low_before, high_after, *product = together(low_before, high_after, *product)
    low_far, high_far = shift(low_before, up, down), shift(high_after, back_up, back_down)
    return prepared, product, (low_before, high_after), (high_before, low_after), (low_far, high_far)


LOW, HIGH = NEAR[:2], NEAR[2:]
STAGES = (
    [[(a, 0) for a in LOW], [(a, 0) for a in HIGH]],
    [[(a, -1) for a in LOW], [(a, 1) for a in HIGH]],
    [[(a, -1) for a in HIGH], [(a, 1) for a in LOW]],
    [[(a, -2) for a in LOW], [(a, 2) for a in HIGH]],
)
ORDER = [block for stage in STAGES for piece in stage for block in piece]
STAGE_ROWS = [sum(len(piece) for piece in stage) * BLOCK for stage in STAGES]
SENDS = (1, 1, 2, 2)


def wrap(step):
    return -2 if step == 2 else step


def slot(block):
    at = ORDER.index(block) * BLOCK
    for stage, rows in enumerate(STAGE_ROWS):
        if at < rows:
            return stage, at
        at -= rows


def twin(block):
    other = (wrap(-block[1]), wrap(-block[0]))
    return next(b for b in ORDER if (wrap(b[0]), wrap(b[1])) == other)


def stage_of(block):
    return max(slot(block)[0], slot(twin(block))[0])


EARLY = sorted((block for block in ORDER if stage_of(block) < 3), key=lambda block: stage_of(block) > 1)
LATE = [block for block in ORDER if stage_of(block) == 3]


def place_here():
    row = lax.axis_index("rows")
    return row // (NY * NX), (row // NX) & (NY - 1), row & (NX - 1), lax.axis_index("feat")


def depth(core, block):
    return jnp.where(core == 0, block[1], -block[0])


def first_rows(place, block):
    z, y, x, core = place[0], place[1], place[2], place[3] & 1
    dz = depth(core, block)
    dy = jnp.where(core == 0, block[0], -block[1])
    row = ((z + dz) & (NZ - 1)) * (NY * NX) + ((y + dy) & (NY - 1)) * NX + x
    return [pl.multiple_of((row ^ (NZ // 2 * NY * NX * (part % 2) + part // 2)) * SHARD, SHARD) for part in range(4)]


def twin_rows(place, block):
    core = place[3] & 1
    stage, start = slot(twin(block))
    each = STAGE_ROWS[stage] // SENDS[stage]
    parts = [start % each + part * SHARD for part in range(4)]
    if 2 in map(abs, block + twin(block)):
        away = (((depth(core, block) - depth(1 - core, twin(block))) >> 2) & 1) * SHARD
        parts = [pl.multiple_of(row ^ away, SHARD) for row in parts]
    return sum(SENDS[:stage]) + start // each, parts


def split3(value):
    high = value.astype(jnp.bfloat16)
    rest = value - high.astype(jnp.float32)
    middle = rest.astype(jnp.bfloat16)
    low = (rest - middle.astype(jnp.float32)).astype(jnp.bfloat16)
    return [high, middle, low]


def copy_kernel(from_ref, to_ref):
    to_ref[...] = from_ref[...]


def prepare_kernel(train_ref, turned_ref, sums_ref):
    me = lax.axis_index("feat")
    for k, mask in enumerate((0, 2, 1, 3)):
        start = pl.multiple_of((me ^ mask) * 256, 256)
        for j in range(0, 2048, 512):
            block = train_ref[pl.ds(start, 256), j : j + 512].T
            turned_ref[k, j : j + 512, :] = block
            wide = block.astype(jnp.float32)
            part = jnp.sum(wide * wide, axis=0, keepdims=True)
            if j == 0:
                sums_ref[k : k + 1, :] = part
            else:
                sums_ref[k : k + 1, :] += part


def condition(pieces, precond_ref, sums_ref, rounded_ref):
    base = 0
    for piece in pieces:
        rows = piece.shape[0]
        here = slice(base, base + rows)
        squares = jnp.zeros((rows, 128), jnp.float32)
        for k in range(8):
            columns = slice(k * 256, (k + 1) * 256)
            value = jnp.dot(piece[:, columns], precond_ref[k], preferred_element_type=jnp.float32)
            rounded_ref[here, columns] = value.astype(jnp.bfloat16)
            value = value * value
            squares += value[:, :128] + value[:, 128:]
        sums_ref[here, :] = squares
        base += rows


def multiply(rounded_ref, turned_ref, refs, first):
    each = rounded_ref.shape[0] // len(refs)
    for k in range(2):
        value = jnp.dot(rounded_ref[...], turned_ref[first + k], preferred_element_type=jnp.float32)
        for n, ref in enumerate(refs):
            ref[:each, k * 256 : (k + 1) * 256] = value[n * each : (n + 1) * each].astype(ref.dtype)


def products_kernel(turned_ref, precond_ref, low, high, keep_ref, *refs):
    *send_refs, sums_ref, rounded_ref = refs
    condition((low, high), precond_ref, sums_ref, rounded_ref)
    multiply(rounded_ref, turned_ref, send_refs, 2)
    multiply(rounded_ref, turned_ref, [keep_ref], 0)


def sent_kernel(turned_ref, precond_ref, low, high, rounded_ref, send_low, send_high, sums_ref):
    condition((low, high), precond_ref, sums_ref, rounded_ref)
    multiply(rounded_ref, turned_ref, [send_low, send_high], 2)


def kept_kernel(turned_ref, rounded_ref, keep_ref):
    multiply(rounded_ref, turned_ref, [keep_ref], 0)


def last_sent_kernel(
    turned_ref, precond_ref, low, high, sums0, sums1, sums2, train_ref, rounded_ref, send_low, send_high, lanes_ref, sums3, all_sums
):
    condition((low, high), precond_ref, sums3, rounded_ref)
    multiply(rounded_ref, turned_ref, [send_low, send_high], 2)
    sums = (sums0, sums1, sums2, sums3)
    place = place_here()
    for block in ORDER:
        stage, at = slot(block)
        for part, row in enumerate(first_rows(place, block)):
            here = slice(at + part * SHARD, at + (part + 1) * SHARD)
            all_sums[pl.ds(row, SHARD), :] = sums[stage][here, :]
    lanes = jnp.sum(all_sums[...].T, axis=0, keepdims=True)
    lanes_ref[...] = lanes
    extra = split3(lanes[:, :512]) + split3(lanes[:, 512:])
    extra += split3(jnp.concatenate([train_ref[2:3, :], train_ref[3:4, :]], axis=1))
    extra.append(jnp.zeros((SHARD - len(extra), 512), jnp.bfloat16))
    send_high[low.shape[0] :, :] = jnp.concatenate(extra, axis=0)


def add_blocks(blocks, keeps, gots, mine_ref, send_ref, at=0):
    first = at
    place = place_here()
    for block in blocks:
        stage, base = slot(block)
        there, rows = twin_rows(place, block)
        for part, row in enumerate(rows):
            own = keeps[stage][base + part * SHARD : base + (part + 1) * SHARD, :]
            total = own + gots[there][pl.ds(row, SHARD), :].astype(jnp.float32)
            mine_ref[at : at + SHARD, :] = total[:, :256]
            send_ref[at - first : at - first + SHARD, :] = total[:, 256:].astype(jnp.bfloat16)
            at += SHARD


def early_kernel(*refs):
    keeps, gots = refs[: len(STAGES) - 1], refs[len(STAGES) - 1 : -2]
    add_blocks(EARLY, keeps, gots, *refs[-2:])


def late_kernel(*refs):
    first, last = len(STAGES), len(STAGES) + sum(SENDS)
    keeps, gots, rest = refs[:first], refs[first:last], refs[last:]
    lanes_ref, train_ref, mine_ref, send_low, send_high, lanes2_ref, train2_ref = rest
    add_blocks(LATE[:4], keeps, gots, mine_ref, send_low)
    add_blocks(LATE[4:], keeps, gots, mine_ref, send_high, 4 * BLOCK)
    got = gots[-1][keeps[-1].shape[0] // 2 :, :].astype(jnp.float32)
    extra = []
    for j in range(2):
        columns = slice(j * 512, (j + 1) * 512)
        total = lanes_ref[:, columns] + sum3(got, 3 * j)
        lanes2_ref[:, columns] = total
        extra += split3(total[:, :256]) + split3(total[:, 256:])
    train = sum3(got, 6)
    train2_ref[...] = train_ref[0:1, :] + train[:, :256]
    extra += split3(train_ref[1:2, :] + train[:, 256:])
    extra.append(jnp.zeros((SHARD - len(extra), 256), jnp.bfloat16))
    send_high[len(LATE[4:]) * BLOCK :, :] = jnp.concatenate(extra, axis=0)


def sum3(rows, at):
    return rows[at : at + 1] + (rows[at + 1 : at + 2] + rows[at + 2 : at + 3])


def merge_kernel(mine0, got0, all_ref):
    all_ref[...] = mine0[...] + got0[...].astype(jnp.float32)


def finish_kernel(early_ref, mine1, got1, got2, lanes_ref, train_ref, out_ref, scale_ref, sums_ref, sem):
    split = got1.shape[0]
    late = mine1.shape[0]
    got = got2[late - split :, :].astype(jnp.float32)
    query = lanes_ref[...] + jnp.concatenate([sum3(got, 3 * j) for j in range(4)], axis=1)
    query = 1.0 / jnp.sqrt(query + EPS)
    for i in range(0, 1024, 128):
        scale_ref[i : i + 128, :] = jnp.broadcast_to(query[:, i : i + 128], (128, 128)).T
    train = (1.0 / jnp.sqrt(train_ref[...] + sum3(got, 12) + EPS)) * math.sqrt(F)
    at = 0
    place = place_here()
    for block in EARLY + LATE:
        for row in first_rows(place, block):
            base = at - len(EARLY) * BLOCK
            if base < 0:
                total = early_ref[at : at + SHARD, :]
            else:
                other = got1[base : base + SHARD, :] if base < split else got2[base - split : base - split + SHARD, :]
                total = mine1[base : base + SHARD, :] + other.astype(jnp.float32)
            rows = pl.ds(row, SHARD)
            scale = scale_ref[rows, :]
            for j in range(0, 256, 128):
                sums_ref[at : at + SHARD, j : j + 128] = total[:, j : j + 128] * scale * train[:, j : j + 128]
            pltpu.make_async_copy(sums_ref.at[at : at + SHARD, :], out_ref.at[rows, :], sem).start()
            at += SHARD
    pltpu.make_async_copy(sums_ref, out_ref, sem).wait()


def call(kernel, outs, inputs, scratch=(), out_spec=VMEM):
    return pl.pallas_call(
        kernel,
        out_shape=[jax.ShapeDtypeStruct(s, d) for s, d in outs],
        in_specs=[VMEM] * len(inputs),
        out_specs=[out_spec] * len(outs),
        scratch_shapes=list(scratch),
        compiler_params=pltpu.CompilerParams(vmem_limit_bytes=24 * MIB),
        cost_estimate=pl.CostEstimate(flops=1, bytes_accessed=1, transcendentals=0),
    )(*inputs)


def on_device(query_grads, train_grads, precond):
    f32, bf16 = jnp.float32, jnp.bfloat16

    def prepare(four):
        train, _ = together(train_grads, four)
        return call(
            prepare_kernel,
            [((4, 2048, 256), bf16), ((4, 256), f32)],
            [train],
            )

    def product(pieces, prepared, sends=1):
        rows = sum(piece.shape[0] for piece in pieces)
        return call(
            products_kernel,
            [((rows, 512), f32), *[((rows // sends, 512), bf16)] * sends, ((rows, 128), f32)],
            [prepared[0], precond, *pieces],
            scratch=[pltpu.VMEM((rows, 2048), bf16)],
        )

    prepared, done, *stages, last = gather(query_grads, prepare, product)
    turned, train_sums = prepared
    keep, send, squares = done
    keeps, sums = [keep], [squares]
    *pieces, _ = together(*stages[0], squares)
    keep, send1, squares = product(pieces, prepared)
    keeps.append(keep)
    sums.append(squares)
    send, _ = together(send, squares)
    gots = [across(send, 1), across(send1, 1)]
    rows = STAGE_ROWS[2]
    *pieces, _, _ = together(*stages[1], squares, gots[0])
    rounded, send_low, send_high, squares = call(
        sent_kernel,
        [((rows, 2048), bf16), *[((rows // 2, 512), bf16)] * 2, ((rows, 128), f32)],
        [turned, precond, *pieces],
    )
    sums.append(squares)
    early = len(EARLY) * BLOCK
    late = len(LATE) * BLOCK
    keeps.append(call(kept_kernel, [((rows, 512), f32)], [turned, rounded])[0])
    gots += [across(send_low, 1), across(send_high, 1)]
    mine0, send = call(early_kernel, [((early, 256), f32), ((early, 256), bf16)], [*keeps, *gots])
    got0 = across(send, 2)
    low, high, _ = together(*last, send)
    rows = STAGE_ROWS[-1]
    rounded, send_low, send_high, lanes = call(
        last_sent_kernel,
        [((rows, 2048), bf16), ((rows // 2, 512), bf16), ((rows // 2 + SHARD, 512), bf16), ((1, 1024), f32)],
        [turned, precond, low, high, *sums, train_sums],
        scratch=[pltpu.VMEM((rows, 128), f32), pltpu.VMEM((1024, 128), f32)],
    )
    keeps.append(call(kept_kernel, [((rows, 512), f32)], [turned, rounded])[0])
    gots += [across(send_low, 1), across(send_high, 1)]
    mine1, send_low, send_high, lanes, train = call(
        late_kernel,
        [
            ((late, 256), f32),
            ((4 * BLOCK, 256), bf16),
            ((late - 4 * BLOCK + SHARD, 256), bf16),
            ((1, 1024), f32),
            ((1, 256), f32),
        ],
        [*keeps, *gots, lanes, train_sums],
    )
    got1, got2 = across(send_low, 2), across(send_high, 2)
    merged = call(merge_kernel, [((early, 256), f32)], [mine0, got0])[0]
    return call(
        finish_kernel,
        [((1024, 256), f32)],
        [merged, mine1, got1, got2, lanes, train],
        scratch=[pltpu.VMEM((1024, 128), f32), pltpu.VMEM((1024, 256), f32), pltpu.SemaphoreType.DMA],
        out_spec=pl.BlockSpec(memory_space=pl.ANY),
    )[0]


def solution(mesh):
    in_specs = (P("rows", "feat"), P("rows", "feat"), P("feat", None, None))
    out_specs = P(None, ("rows", "feat"))
    return jax.shard_map(
        on_device, mesh=mesh, in_specs=in_specs, out_specs=out_specs, check_vma=False
    )
```
